256 devices in a mesh: dp: 64 (over x, z, core), tensor: 4 (over y).
Axes of the slice: x: 4, y: 4, z: 8, core: 2. Of those that a mesh axis runs over, the one named last changes fastest.
Arguments:
- grads: bfloat16 [64, 256, 28672], P('dp', None, 'tensor'), may hold values from -52 to 52
- error: bfloat16 [64, 256, 28672], P('dp', None, 'tensor'), may hold values from -3 to 3
- q_in: float32 [28672, 32], P('tensor'), may hold values from -6 to 6
Outputs:
- p_basis: float32 [256, 32], replicated
- q_mean: float32 [28672, 32], P('tensor')
- new_error: bfloat16 [64, 256, 28672], P('dp', None, 'tensor')
The draws below stay inside these ranges and needn't reach their ends.
All inputs are finite; a program needn't handle non-finite values.
Results may differ from the reference program's by a relative error of at most 0.0085.
Values sent between devices are 32-bit elements; how exact they have to be, the bound alone decides.
No kernel may reach another device: no remote copies, remote signals or barrier semaphores. Data moves between devices by JAX's collectives and lax.ppermute only.
A program may use at most 64 MiB of HBM per device.

```python
import jax
import jax.numpy as jnp
from jax import lax

FF = 28672
ROWS = 256
R = 32
REPLICAS = 64


def draw_grads(key, part):
    key = jax.random.fold_in(key, 7)
    key_shared, key_own = jax.random.split(key, 2)
    shared = jnp.clip(jax.random.normal(key_shared, (ROWS, FF), jnp.float32), -4.0, 4.0)
    own = jnp.clip(jax.random.normal(key_own, (REPLICAS, ROWS, FF), jnp.float32), -4.0, 4.0)
    return (0.6 * shared + own).astype(jnp.bfloat16)


def level_of(key, dims, pieces, low, largest):
    level, own = 1.0, jax.random.fold_in(key, 6)
    for position, blocks in pieces:
        steps = jnp.exp(jax.random.uniform(jax.random.fold_in(own, position), (blocks,), jnp.float32, low / len(pieces), largest / len(pieces)))
        level = level * jnp.repeat(steps, dims[position] // blocks).reshape([-1 if axis == position else 1 for axis in range(len(dims))])
    return level


def gaussian(stream_key, extent, width, limit, cuts=(), kind=jnp.bfloat16):
    level = level_of(stream_key, extent, cuts, -0.22, 0.18) if cuts else 1.0
    drawn = jax.random.normal(stream_key, extent, jnp.float32) * width * level
    return jnp.minimum(jnp.maximum(drawn, -limit), limit).astype(kind)


def setup_inputs(seed: int = 0) -> dict:
    arg_keys = jax.random.split(jax.random.key(seed), 4)
    return {
        "grads": draw_grads(jax.random.fold_in(arg_keys[3], 71), 0),
        "error": gaussian(arg_keys[1], (REPLICAS, ROWS, FF), 0.5, 3.0, ((0, 64), (2, 4))),
        "q_in": gaussian(arg_keys[2], (FF, R), 1.0, 6.0, ((0, 4),), jnp.float32),
    }


EPS = 1e-06

def orthonormal(p_matrix):
    count = p_matrix.shape[1]
    column_ids = jnp.arange(count).astype(jnp.int32)

    def orth_step(column, built):
        column = jnp.asarray(column).astype(jnp.int32)
        vector = lax.dynamic_slice_in_dim(p_matrix, column, 1, 1)
        below_mask = (column_ids < column).astype(p_matrix.dtype)
        for repeat_pass in range(2):
            coeffs = jnp.dot(built.T, vector, precision=lax.Precision.HIGHEST) * below_mask[:, None]
            vector = vector - jnp.dot(built, coeffs, precision=lax.Precision.HIGHEST)
        vector = vector * lax.rsqrt(jnp.sum(vector * vector) + EPS)
        return lax.dynamic_update_slice_in_dim(built, vector, column, 1)
    return lax.fori_loop(0, count, orth_step, jnp.zeros_like(p_matrix))

def merge_one(grad_block, error_block):
    return (grad_block.astype(jnp.float32) + error_block.astype(jnp.float32)).astype(jnp.bfloat16)

def reference(grads, error, q_in):
    q_half = q_in.astype(jnp.bfloat16)

    def p_step(running, grad_pair):
        merged = merge_one(grad_pair[0], grad_pair[1])
        return (running + jnp.dot(merged, q_half, preferred_element_type=jnp.float32), None)
    p_sum, unused = lax.scan(p_step, jnp.zeros((ROWS, R), jnp.float32), (grads, error))
    p_basis = orthonormal(p_sum)
    p_half = p_basis.astype(jnp.bfloat16)

    def q_step(running, grad_pair):
        merged = merge_one(grad_pair[0], grad_pair[1])
        return (running + jnp.dot(merged.T, p_half, preferred_element_type=jnp.float32), None)
    q_sum, unused = lax.scan(q_step, jnp.zeros((FF, R), jnp.float32), (grads, error))
    q_mean = q_sum / REPLICAS
    approx = jnp.dot(p_basis, q_mean.T, precision=lax.Precision.HIGHEST)

    def rewrite(grad_pair):
        merged = merge_one(grad_pair[0], grad_pair[1])
        return (merged.astype(jnp.float32) - approx).astype(jnp.bfloat16)
    new_error = lax.map(rewrite, (grads, error))
    return (p_basis, q_mean, new_error)
```

```python
import jax
import jax.numpy as jnp
from jax import lax
from jax.experimental import pallas as pl
from jax.experimental.pallas import tpu as pltpu
from jax.sharding import Mesh, PartitionSpec as P

EPS = 1e-06
NX, NZ, NC, NY = 4, 8, 2, 4
ROWS, R, COLS = 256, 32, 7168
HALF = R // NC
GROUP = HALF // NX
PIECE = COLS // NZ
REPLICAS = NX * NZ * NC
STEP = 1024

VMEM = pl.BlockSpec(memory_space=pltpu.VMEM)
SMEM = pl.BlockSpec(memory_space=pltpu.SMEM)


def params(mib):
    return pltpu.CompilerParams(vmem_limit_bytes=mib * 1024 * 1024)


def merge_kernel(core_ref, grads_ref, error_ref, q_ref, merged_ref, keep_ref, send_ref, total_ref):
    step = pl.program_id(0)
    merged = (grads_ref[0].astype(jnp.float32) + error_ref[0].astype(jnp.float32)).astype(jnp.bfloat16)
    merged_ref[...] = merged
    term = lax.dot_general(q_ref[...].astype(jnp.bfloat16), merged, (((1,), (1,)), ((), ())),
                           preferred_element_type=jnp.float32)

    @pl.when(step == 0)
    def _():
        total_ref[...] = term

    @pl.when(step > 0)
    def _():
        total_ref[...] += term

    @pl.when(step == pl.num_programs(0) - 1)
    def _():
        first = core_ref[0] == 0
        low, high = total_ref[:HALF], total_ref[HALF:]
        keep_ref[...] = jnp.where(first, low, high)
        send_ref[...] = jnp.where(first, high, low)


def merge(core, grads, error, q_t):
    return pl.pallas_call(
        merge_kernel,
        grid=(COLS // STEP,),
        in_specs=[
            SMEM,
            pl.BlockSpec((1, ROWS, STEP), lambda i: (0, 0, i)),
            pl.BlockSpec((1, ROWS, STEP), lambda i: (0, 0, i)),
            pl.BlockSpec((R, STEP), lambda i: (0, i)),
        ],
        out_specs=[
            pl.BlockSpec((ROWS, STEP), lambda i: (0, i)),
            pl.BlockSpec((HALF, ROWS), lambda i: (0, 0)),
            pl.BlockSpec((HALF, ROWS), lambda i: (0, 0)),
        ],
        out_shape=[
            jax.ShapeDtypeStruct((ROWS, COLS), jnp.bfloat16),
            jax.ShapeDtypeStruct((HALF, ROWS), jnp.float32),
            jax.ShapeDtypeStruct((HALF, ROWS), jnp.float32),
        ],
        scratch_shapes=[pltpu.VMEM((R, ROWS), jnp.float32)],
        compiler_params=params(32),
        name="merge",
    )(core, grads, error, q_t)


def orthonormal_kernel(core_ref, own_ref, other_ref, basis_ref, half_ref):
    first = core_ref[0] == 0
    own, other = own_ref[...], other_ref[...]
    low, high = jnp.where(first, own, other), jnp.where(first, other, own)
    tiles = [low[:8], low[8:], high[:8], high[8:]]
    left = list(tiles)
    basis = [jnp.zeros_like(tile) for tile in tiles]
    rows = lax.broadcasted_iota(jnp.int32, (8, 1), 0)
    for column in range(R):
        tile, row = divmod(column, 8)
        vector = left[tile][row:row + 1]
        if column > 0:
            built = (column - 1) // 8 + 1
            taken = None
            for part in basis[:built]:
                term = jnp.sum(part * vector, axis=1, keepdims=True) * part
                taken = term if taken is None else taken + term
            vector = vector - jnp.sum(taken, axis=0, keepdims=True)
        vector = vector * lax.rsqrt(jnp.sum(vector * vector, axis=1, keepdims=True) + EPS)
        basis[tile] = jnp.where(rows == row, vector, basis[tile])
        for later in range((column + 1) // 8, R // 8):
            coeffs = jnp.sum(tiles[later] * vector, axis=1, keepdims=True)
            left[later] = left[later] - coeffs * vector
    result = jnp.concatenate(basis, axis=0)
    basis_ref[...] = result
    half_ref[...] = result.astype(jnp.bfloat16)


def orthonormal(core, own, other):
    return pl.pallas_call(
        orthonormal_kernel,
        in_specs=[SMEM, VMEM, VMEM],
        out_specs=[VMEM, VMEM],
        out_shape=[
            jax.ShapeDtypeStruct((R, ROWS), jnp.float32),
            jax.ShapeDtypeStruct((R, ROWS), jnp.bfloat16),
        ],
        name="orthonormal",
    )(core, own, other)


def right_kernel(core_ref, half_ref, merged_ref, keep_ref, send_ref):
    first = core_ref[0] == 0
    term = jnp.dot(half_ref[...], merged_ref[...], preferred_element_type=jnp.float32)
    keep_ref[...] = jnp.where(first, term[:HALF], term[HALF:])
    send_ref[...] = jnp.where(first, term[HALF:], term[:HALF])


def right(core, p_half, merged):
    return pl.pallas_call(
        right_kernel,
        grid=(COLS // STEP,),
        in_specs=[
            SMEM,
            pl.BlockSpec((R, ROWS), lambda i: (0, 0)),
            pl.BlockSpec((ROWS, STEP), lambda i: (0, i)),
        ],
        out_specs=[pl.BlockSpec((HALF, STEP), lambda i: (0, i))] * 2,
        out_shape=[jax.ShapeDtypeStruct((HALF, COLS), jnp.float32)] * 2,
        compiler_params=params(32),
        name="right",
    )(core, p_half, merged)


def pieces_kernel(keep_ref, got_ref, out_ref):
    for z in range(NZ):
        columns = slice(z * PIECE, (z + 1) * PIECE)
        both = keep_ref[:, columns] + got_ref[:, columns]
        for x in range(NX):
            out_ref[x * NZ + z] = both[x * GROUP:(x + 1) * GROUP]


def pieces(keep, got):
    return pl.pallas_call(
        pieces_kernel,
        in_specs=[VMEM, VMEM],
        out_specs=VMEM,
        out_shape=jax.ShapeDtypeStruct((NX * NZ, GROUP, PIECE), jnp.float32),
        compiler_params=params(16),
        name="pieces",
    )(keep, got)


def mean_kernel(terms_ref, out_ref):
    total = terms_ref[0]
    for i in range(1, NX * NZ):
        total = total + terms_ref[i]
    total = total * (1.0 / REPLICAS)
    for i in range(NX * NZ):
        out_ref[i] = total


def mean(terms):
    return pl.pallas_call(
        mean_kernel,
        in_specs=[VMEM],
        out_specs=VMEM,
        out_shape=jax.ShapeDtypeStruct((NX * NZ, GROUP, PIECE), jnp.float32),
        compiler_params=params(16),
        name="mean",
    )(terms)


def split3(value):
    first = value.astype(jnp.bfloat16)
    rest = value - first.astype(jnp.float32)
    second = rest.astype(jnp.bfloat16)
    third = (rest - second.astype(jnp.float32)).astype(jnp.bfloat16)
    return first, second, third


def rewrite_kernel(core_ref, own_ref, other_ref, basis_ref, merged_ref, mean_ref, error_ref):
    first = core_ref[0] == 0
    own = jnp.concatenate([own_ref[x, 0] for x in range(NX)], axis=0)
    other = jnp.concatenate([other_ref[x, 0] for x in range(NX)], axis=0)
    q_mean = jnp.concatenate([jnp.where(first, own, other), jnp.where(first, other, own)], axis=0)
    mean_ref[...] = q_mean
    q1, q2, q3 = split3(q_mean)
    p1, p2, p3 = split3(basis_ref[...])
    p_all = jnp.concatenate([p1, p1, p2, p2, p1, p3], axis=0)
    q_all = jnp.concatenate([q1, q2, q1, q2, q3, q1], axis=0)
    approx = lax.dot_general(p_all, q_all, (((0,), (0,)), ((), ())), preferred_element_type=jnp.float32)
    error_ref[0] = (merged_ref[...].astype(jnp.float32) - approx).astype(jnp.bfloat16)


def rewrite(core, own, other, basis, merged):
    piece_spec = pl.BlockSpec((NX, 1, GROUP, PIECE), lambda i: (0, i, 0, 0))
    return pl.pallas_call(
        rewrite_kernel,
        grid=(NZ,),
        in_specs=[
            SMEM,
            piece_spec,
            piece_spec,
            pl.BlockSpec((R, ROWS), lambda i: (0, 0)),
            pl.BlockSpec((ROWS, PIECE), lambda i: (0, i)),
        ],
        out_specs=[
            pl.BlockSpec((R, PIECE), lambda i: (0, i)),
            pl.BlockSpec((1, ROWS, PIECE), lambda i: (0, 0, i)),
        ],
        out_shape=[
            jax.ShapeDtypeStruct((R, COLS), jnp.float32),
            jax.ShapeDtypeStruct((1, ROWS, COLS), jnp.bfloat16),
        ],
        compiler_params=params(32),
        name="rewrite",
    )(core, own, other, basis, merged)


def shift(value, axis, size, by):
    return lax.ppermute(value, axis, [(i, (i + by) % size) for i in range(size)])


def swap(value, axis, size):
    return lax.ppermute(value, axis, [(i, i ^ 1) for i in range(size)])


def ring4(value, axis, size, unit):
    across = shift(value, axis, size, 2 * unit)
    left = shift(value, axis, size, unit)
    right = shift(value, axis, size, size - unit)
    return (value + across) + (left + right)


def on_device(grads, error, q_in):
    core = lax.axis_index("c").astype(jnp.int32)[None]
    merged, keep, send = merge(core, grads, error, q_in.T)
    own = keep + swap(send, "c", NC)
    own = ring4(own, "y", NY, 1)
    own = ring4(own, "x", NX, 1)
    own = own + swap(own, "z", NZ)
    own = ring4(own, "z", NZ, 2)
    basis, p_half = orthonormal(core, own, swap(own, "c", NC))

    keep, send = right(core, p_half, merged)
    terms = lax.all_to_all(pieces(keep, swap(send, "c", NC)), ("x", "z"), 0, 0, tiled=True)
    own = lax.all_to_all(mean(terms), ("x", "z"), 0, 0, tiled=True)
    other = swap(own, "c", NC)
    shape = (NX, NZ, GROUP, PIECE)
    q_mean, new_error = rewrite(core, own.reshape(shape), other.reshape(shape), basis, merged)
    return basis.T, q_mean.T, new_error


def solution(mesh):
    fine = Mesh(mesh.devices.reshape(NX, NZ, NC, NY), ("x", "z", "c", "y"))
    replicas = ("x", "z", "c")
    in_specs = (P(replicas, None, "y"), P(replicas, None, "y"), P("y", None))
    out_specs = (P(), P("y", None), P(replicas, None, "y"))
    return jax.shard_map(
        on_device, mesh=fine, in_specs=in_specs, out_specs=out_specs, check_vma=False
    )
```

```python
import jax
import jax.numpy as jnp
from jax import lax
from jax.experimental import pallas as pl
from jax.experimental.pallas import tpu as pltpu
from jax.sharding import Mesh, PartitionSpec as P

EPS = 1e-06
NX, NZ, NC, NY = 4, 8, 2, 4
ROWS, R, COLS = 256, 32, 7168
HALF = R // NC
GROUP = HALF // NX
PIECE = COLS // NZ
REPLICAS = NX * NZ * NC
STEP = 1024

VMEM = pl.BlockSpec(memory_space=pltpu.VMEM)
SMEM = pl.BlockSpec(memory_space=pltpu.SMEM)
HBM = pl.BlockSpec(memory_space=pltpu.HBM)
CHUNK = 512
CHUNKS = COLS // CHUNK
Z_SHIFTS = ((4, 3, 1, None), (-3, 2, -2, -1))


def params(mib):
    return pltpu.CompilerParams(vmem_limit_bytes=mib * 1024 * 1024)


def merge_kernel(grads_ref, error_ref, q_ref, merged_ref, term_ref, g_buf, e_buf, q_buf, g_sem, e_sem, q_sem):
    def copies(i):
        columns = pl.ds(i * CHUNK, CHUNK)
        return (
            pltpu.make_async_copy(grads_ref.at[0, :, columns], g_buf.at[i], g_sem.at[i]),
            pltpu.make_async_copy(error_ref.at[0, :, columns], e_buf.at[i], e_sem.at[i]),
            pltpu.make_async_copy(q_ref.at[:, columns], q_buf.at[i], q_sem.at[i]),
        )

    for i in range(CHUNKS):
        for copy in copies(i):
            copy.start()
    total = jnp.zeros((R, ROWS), jnp.float32)
    for i in range(CHUNKS):
        for copy in copies(i):
            copy.wait()
        merged = (g_buf[i].astype(jnp.float32) + e_buf[i].astype(jnp.float32)).astype(jnp.bfloat16)
        merged_ref[:, i * CHUNK:(i + 1) * CHUNK] = merged
        total += lax.dot_general(q_buf[i].astype(jnp.bfloat16), merged, (((1,), (1,)), ((), ())),
                                 preferred_element_type=jnp.float32)
    term_ref[...] = total


def merge(grads, error, q_t):
    return pl.pallas_call(
        merge_kernel,
        in_specs=[HBM, HBM, HBM],
        out_specs=[VMEM, VMEM],
        out_shape=[
            pltpu.VMEM((ROWS, COLS), jnp.bfloat16),
            pltpu.VMEM((R, ROWS), jnp.float32),
        ],
        scratch_shapes=[
            pltpu.VMEM((CHUNKS, ROWS, CHUNK), jnp.bfloat16),
            pltpu.VMEM((CHUNKS, ROWS, CHUNK), jnp.bfloat16),
            pltpu.VMEM((CHUNKS, R, CHUNK), jnp.float32),
            pltpu.SemaphoreType.DMA((CHUNKS,)),
            pltpu.SemaphoreType.DMA((CHUNKS,)),
            pltpu.SemaphoreType.DMA((CHUNKS,)),
        ],
        compiler_params=params(24),
        name="merge",
    )(*(pltpu.with_memory_space_constraint(a, pltpu.HBM) for a in (grads, error, q_t)))


def orthonormal_kernel(core_ref, z_ref, own_ref, *refs):
    mine, theirs = refs[:4], refs[4:8]
    basis_ref, half_ref, ring = refs[8:]
    core, z = core_ref[0], z_ref[0]
    ring[z] = own_ref[...]
    for group, owner in ((mine, core), (theirs, 1 - core)):
        for ref, low, high in zip(group, *Z_SHIFTS):
            if low is None:
                @pl.when(owner == 1)
                def _():
                    ring[(z - high + NZ) % NZ] = ref[...]
            else:
                ring[(z - jnp.where(owner == 0, low, high) + NZ) % NZ] = ref[...]
    total = (ring[0] + ring[1]) + (ring[2] + ring[3])
    total = total + ((ring[4] + ring[5]) + (ring[6] + ring[7]))

    tiles = [total[8 * i:8 * i + 8] for i in range(R // 8)]
    left = list(tiles)
    basis = [jnp.zeros_like(tile) for tile in tiles]
    rows = lax.broadcasted_iota(jnp.int32, (8, 1), 0)
    for column in range(R):
        tile, row = divmod(column, 8)
        vector = left[tile][row:row + 1]
        if column > 0:
            built = (column - 1) // 8 + 1
            taken = None
            for part in basis[:built]:
                term = jnp.sum(part * vector, axis=1, keepdims=True) * part
                taken = term if taken is None else taken + term
            vector = vector - jnp.sum(taken, axis=0, keepdims=True)
        products = [jnp.sum(tiles[later] * vector, axis=1, keepdims=True) for later in range((column + 1) // 8, R // 8)]
        scale = lax.rsqrt(jnp.sum(vector * vector, axis=1, keepdims=True) + EPS)
        basis[tile] = jnp.where(rows == row, vector * scale, basis[tile])
        square = scale * scale
        for later, product in zip(range((column + 1) // 8, R // 8), products):
            left[later] = left[later] - (product * square) * vector
    result = jnp.concatenate(basis, axis=0)
    basis_ref[...] = result
    half_ref[...] = result.astype(jnp.bfloat16)


def orthonormal(core, z, own, mine, theirs):
    return pl.pallas_call(
        orthonormal_kernel,
        in_specs=[SMEM, SMEM] + [VMEM] * 9,
        out_specs=[VMEM, VMEM],
        out_shape=[
            pltpu.VMEM((R, ROWS), jnp.float32),
            pltpu.VMEM((R, ROWS), jnp.bfloat16),
        ],
        scratch_shapes=[pltpu.VMEM((NZ, R, ROWS), jnp.float32)],
        compiler_params=params(16),
        name="orthonormal",
    )(core, z, own, *mine, *theirs)


def right_kernel(core_ref, half_ref, merged_ref, keep_ref, send_ref):
    first = core_ref[0] == 0
    half = half_ref[...]
    for i in range(COLS // STEP):
        columns = slice(i * STEP, (i + 1) * STEP)
        term = jnp.dot(half, merged_ref[:, columns], preferred_element_type=jnp.float32)
        keep_ref[:, columns] = jnp.where(first, term[:HALF], term[HALF:])
        send_ref[:, columns] = jnp.where(first, term[HALF:], term[:HALF])


def right(core, p_half, merged):
    return pl.pallas_call(
        right_kernel,
        in_specs=[SMEM, VMEM, VMEM],
        out_specs=[VMEM, VMEM],
        out_shape=[pltpu.VMEM((HALF, COLS), jnp.float32)] * 2,
        compiler_params=params(16),
        name="right",
    )(core, p_half, merged)


def pieces_kernel(keep_ref, got_ref, out_ref):
    for z in range(NZ):
        columns = slice(z * PIECE, (z + 1) * PIECE)
        both = keep_ref[:, columns] + got_ref[:, columns]
        for x in range(NX):
            out_ref[x * NZ + z] = both[x * GROUP:(x + 1) * GROUP]


def pieces(keep, got):
    return pl.pallas_call(
        pieces_kernel,
        in_specs=[VMEM, VMEM],
        out_specs=VMEM,
        out_shape=pltpu.VMEM((NX * NZ, GROUP, PIECE), jnp.float32),
        compiler_params=params(16),
        name="pieces",
    )(keep, got)


def mean_kernel(terms_ref, out_ref):
    total = terms_ref[0]
    for i in range(1, NX * NZ):
        total = total + terms_ref[i]
    total = total * (1.0 / REPLICAS)
    for i in range(NX * NZ):
        out_ref[i] = total


def mean(terms):
    return pl.pallas_call(
        mean_kernel,
        in_specs=[VMEM],
        out_specs=VMEM,
        out_shape=pltpu.VMEM((NX * NZ, GROUP, PIECE), jnp.float32),
        compiler_params=params(16),
        name="mean",
    )(terms)


def split3(value):
    first = value.astype(jnp.bfloat16)
    rest = value - first.astype(jnp.float32)
    second = rest.astype(jnp.bfloat16)
    third = (rest - second.astype(jnp.float32)).astype(jnp.bfloat16)
    return first, second, third


def rewrite_kernel(core_ref, own_ref, other_ref, basis_ref, merged_ref, mean_ref, error_ref,
                   mean_buf, error_buf, mean_sem, error_sem):
    first = core_ref[0] == 0
    p1, p2, p3 = split3(basis_ref[...])
    p_all = jnp.concatenate([p1, p1, p2, p2, p1, p3], axis=0).T
    copies = []
    for z in range(NZ):
        columns = slice(z * PIECE, (z + 1) * PIECE)
        own = jnp.concatenate([own_ref[x * NZ + z] for x in range(NX)], axis=0)
        other = jnp.concatenate([other_ref[x * NZ + z] for x in range(NX)], axis=0)
        q_mean = jnp.concatenate([jnp.where(first, own, other), jnp.where(first, other, own)], axis=0)
        mean_buf[z] = q_mean
        copies.append(pltpu.make_async_copy(mean_buf.at[z], mean_ref.at[:, columns], mean_sem.at[z]))
        copies[-1].start()
        q1, q2, q3 = split3(q_mean)
        q_all = jnp.concatenate([q1, q2, q1, q2, q3, q1], axis=0)
        approx = jnp.dot(p_all, q_all, preferred_element_type=jnp.float32)
        error_buf[z] = (merged_ref[:, columns].astype(jnp.float32) - approx).astype(jnp.bfloat16)
        copies.append(pltpu.make_async_copy(error_buf.at[z], error_ref.at[0, :, columns], error_sem.at[z]))
        copies[-1].start()
    for copy in copies:
        copy.wait()


def rewrite(core, own, other, basis, merged):
    return pl.pallas_call(
        rewrite_kernel,
        in_specs=[SMEM, VMEM, VMEM, VMEM, VMEM],
        out_specs=[HBM, HBM],
        out_shape=[
            pltpu.HBM((R, COLS), jnp.float32),
            pltpu.HBM((1, ROWS, COLS), jnp.bfloat16),
        ],
        scratch_shapes=[
            pltpu.VMEM((NZ, R, PIECE), jnp.float32),
            pltpu.VMEM((NZ, ROWS, PIECE), jnp.bfloat16),
            pltpu.SemaphoreType.DMA((NZ,)),
            pltpu.SemaphoreType.DMA((NZ,)),
        ],
        compiler_params=params(24),
        name="rewrite",
    )(core, own, other, basis, merged)


def shift(value, axis, size, by):
    return lax.ppermute(value, axis, [(i, (i + by) % size) for i in range(size)])


def swap(value, axis, size):
    return lax.ppermute(value, axis, [(i, i ^ 1) for i in range(size)])


def ring4(value, axis, size, unit):
    across = shift(value, axis, size, 2 * unit)
    left = shift(value, axis, size, unit)
    right = shift(value, axis, size, size - unit)
    return (value + across) + (left + right)


def z_round(value, low, high):
    pairs = []
    for z in range(NZ):
        for core, by in ((0, low), (1, high)):
            if by is not None:
                pairs.append((z * NC + core, (z + by) % NZ * NC + core))
    return lax.ppermute(value, ("z", "c"), pairs)


def on_device(grads, error, q_in):
    core = lax.axis_index("c").astype(jnp.int32)[None]
    z = lax.axis_index("z").astype(jnp.int32)[None]
    merged, term = merge(grads, error, q_in.T)
    own = term + swap(term, "c", NC)
    own = ring4(own, "y", NY, 1)
    own = ring4(own, "x", NX, 1)
    mine = [z_round(own, low, high) for low, high in zip(*Z_SHIFTS)]
    theirs = [swap(value, "c", NC) for value in mine]
    basis, p_half = orthonormal(core, z, own, mine, theirs)

    keep, send = right(core, p_half, merged)
    terms = lax.all_to_all(pieces(keep, swap(send, "c", NC)), ("x", "z"), 0, 0, tiled=True)
    own = lax.all_to_all(mean(terms), ("x", "z"), 0, 0, tiled=True)
    q_mean, new_error = rewrite(core, own, swap(own, "c", NC), basis, merged)
    return basis.T, q_mean.T, new_error


def solution(mesh):
    fine = Mesh(mesh.devices.reshape(NX, NZ, NC, NY), ("x", "z", "c", "y"))
    replicas = ("x", "z", "c")
    in_specs = (P(replicas, None, "y"), P(replicas, None, "y"), P("y", None))
    out_specs = (P(), P("y", None), P(replicas, None, "y"))
    return jax.shard_map(
        on_device, mesh=fine, in_specs=in_specs, out_specs=out_specs, check_vma=False
    )
```

```python
import jax
import jax.numpy as jnp
from jax import lax
from jax.experimental import pallas as pl
from jax.experimental.pallas import tpu as pltpu
from jax.sharding import Mesh, PartitionSpec as P

EPS = 1e-06
NX, NZ, NC, NY = 4, 8, 2, 4
ROWS, R, COLS = 256, 32, 7168
GROUP = R // NZ
BLOCK = COLS // NX
SLOTS = NZ // NC
REPLICAS = NX * NZ * NC

VMEM = pl.BlockSpec(memory_space=pltpu.VMEM)
HBM = pl.BlockSpec(memory_space=pltpu.HBM)
CHUNK = 512
CHUNKS = COLS // CHUNK
Z_SHIFTS = ((4, 3, 1, 0), (-3, 2, -2, -1))


def params(mib):
    return pltpu.CompilerParams(vmem_limit_bytes=mib * 1024 * 1024)


def merge_kernel(grads_ref, error_ref, q_ref, merged_ref, term_ref, g_buf, e_buf, q_buf, g_sem, e_sem, q_sem):
    def copies(i):
        columns = pl.ds(i * CHUNK, CHUNK)
        return (
            pltpu.make_async_copy(grads_ref.at[0, :, columns], g_buf.at[i], g_sem.at[i]),
            pltpu.make_async_copy(error_ref.at[0, :, columns], e_buf.at[i], e_sem.at[i]),
            pltpu.make_async_copy(q_ref.at[:, columns], q_buf.at[i], q_sem.at[i]),
        )

    for i in range(CHUNKS):
        for copy in copies(i):
            copy.start()
    total = jnp.zeros((R, ROWS), jnp.float32)
    for i in range(CHUNKS):
        for copy in copies(i):
            copy.wait()
        merged = (g_buf[i].astype(jnp.float32) + e_buf[i].astype(jnp.float32)).astype(jnp.bfloat16)
        merged_ref[:, i * CHUNK:(i + 1) * CHUNK] = merged
        total += lax.dot_general(q_buf[i].astype(jnp.bfloat16), merged, (((1,), (1,)), ((), ())),
                                 preferred_element_type=jnp.float32)
    term_ref[...] = total


def merge(grads, error, q_t):
    return pl.pallas_call(
        merge_kernel,
        in_specs=[HBM, HBM, HBM],
        out_specs=[VMEM, VMEM],
        out_shape=[
            pltpu.VMEM((ROWS, COLS), jnp.bfloat16),
            pltpu.VMEM((R, ROWS), jnp.float32),
        ],
        scratch_shapes=[
            pltpu.VMEM((CHUNKS, ROWS, CHUNK), jnp.bfloat16),
            pltpu.VMEM((CHUNKS, ROWS, CHUNK), jnp.bfloat16),
            pltpu.VMEM((CHUNKS, R, CHUNK), jnp.float32),
            pltpu.SemaphoreType.DMA((CHUNKS,)),
            pltpu.SemaphoreType.DMA((CHUNKS,)),
            pltpu.SemaphoreType.DMA((CHUNKS,)),
        ],
        compiler_params=params(24),
        name="merge",
    )(*(pltpu.with_memory_space_constraint(a, pltpu.HBM) for a in (grads, error, q_t)))


def z_at(core, slot, sign):
    low, high = Z_SHIFTS[0][slot], Z_SHIFTS[1][slot]
    return (lax.axis_index("z") + jnp.where(core == 0, sign * low, sign * high) + NZ) % NZ


def orthonormal_kernel(own_ref, *refs):
    mine, theirs = refs[:SLOTS], refs[SLOTS:2 * SLOTS]
    basis_ref, half_ref, ring = refs[2 * SLOTS:]
    core = lax.axis_index("c")
    for group, owner in ((mine, core), (theirs, 1 - core)):
        for slot, ref in enumerate(group):
            ring[z_at(owner, slot, -1)] = ref[...]
    ring[lax.axis_index("z")] = own_ref[...]
    total = (ring[0] + ring[1]) + (ring[2] + ring[3])
    total = total + ((ring[4] + ring[5]) + (ring[6] + ring[7]))

    tiles = [total[8 * i:8 * i + 8] for i in range(R // 8)]
    left = list(tiles)
    basis = [jnp.zeros_like(tile) for tile in tiles]
    rows = lax.broadcasted_iota(jnp.int32, (8, 1), 0)
    for column in range(R):
        tile, row = divmod(column, 8)
        vector = left[tile][row:row + 1]
        if column > 0:
            built = (column - 1) // 8 + 1
            taken = None
            for part in basis[:built]:
                term = jnp.sum(part * vector, axis=1, keepdims=True) * part
                taken = term if taken is None else taken + term
            vector = vector - jnp.sum(taken, axis=0, keepdims=True)
        products = [jnp.sum(tiles[later] * vector, axis=1, keepdims=True) for later in range((column + 1) // 8, R // 8)]
        scale = lax.rsqrt(jnp.sum(vector * vector, axis=1, keepdims=True) + EPS)
        basis[tile] = jnp.where(rows == row, vector * scale, basis[tile])
        square = scale * scale
        for later, product in zip(range((column + 1) // 8, R // 8), products):
            left[later] = left[later] - (product * square) * vector
    result = jnp.concatenate(basis, axis=0)
    basis_ref[...] = result
    half_ref[...] = result.astype(jnp.bfloat16)


def small(kernel, out, count, name, *args, scratch=()):
    return pl.pallas_call(
        kernel,
        in_specs=[VMEM] * len(args),
        out_specs=[VMEM] * count,
        out_shape=[pltpu.VMEM(out, jnp.float32)] * count,
        scratch_shapes=list(scratch),
        compiler_params=params(16),
        name=name,
    )(*args)


def orthonormal(own, mine, theirs):
    return pl.pallas_call(
        orthonormal_kernel,
        in_specs=[VMEM] * (1 + 2 * SLOTS),
        out_specs=[VMEM, VMEM],
        out_shape=[
            pltpu.VMEM((R, ROWS), jnp.float32),
            pltpu.VMEM((R, ROWS), jnp.bfloat16),
        ],
        scratch_shapes=[pltpu.VMEM((NZ, R, ROWS), jnp.float32)],
        compiler_params=params(16),
        name="orthonormal",
    )(own, *mine, *theirs)


def right_kernel(half_ref, merged_ref, keep_ref, send_ref, groups):
    half = half_ref[...]
    core, x = lax.axis_index("c"), lax.axis_index("x")
    for block in range(NX):
        term = jnp.dot(half, merged_ref[:, block * BLOCK:(block + 1) * BLOCK], preferred_element_type=jnp.float32)
        for group in range(NZ):
            groups[block, group] = term[group * GROUP:(group + 1) * GROUP]
    for ahead in range(NX):
        block = (x + ahead) % NX
        for slot in range(SLOTS):
            keep_ref[ahead, slot] = groups[block, z_at(core, slot, 1)]
            send_ref[ahead, slot] = groups[block, z_at(1 - core, slot, 1)]


def chip_sum_kernel(keep_ref, got_ref, *outs):
    for ahead, out in enumerate(outs):
        out[...] = keep_ref[ahead] + got_ref[ahead]


def x_sum_kernel(own_ref, one_ref, two_ref, three_ref, *outs):
    for slot, out in enumerate(outs):
        out[...] = (own_ref[slot] + two_ref[slot]) + (one_ref[slot] + three_ref[slot])


def z_sum_kernel(own_ref, *refs):
    *got, out_ref = refs
    last = jnp.where(lax.axis_index("c") == 0, own_ref[...], got[-1][...])
    out_ref[...] = (got[0][...] + got[1][...]) + (got[2][...] + last)


def mean_kernel(one_ref, other_ref, out_ref):
    out_ref[...] = (one_ref[...] + other_ref[...]) * (1.0 / REPLICAS)


def collect_kernel(own_ref, *refs):
    *got, out_ref = refs
    for slot in range(SLOTS - 1):
        out_ref[slot] = got[slot][...]
    out_ref[SLOTS - 1] = jnp.where(lax.axis_index("c") == 0, own_ref[...], got[-1][...])


def split3(value):
    first = value.astype(jnp.bfloat16)
    rest = value - first.astype(jnp.float32)
    second = rest.astype(jnp.bfloat16)
    third = (rest - second.astype(jnp.float32)).astype(jnp.bfloat16)
    return first, second, third


def rewrite_kernel(*refs):
    own, other = refs[:NX], refs[NX:2 * NX]
    basis_ref, merged_ref, mean_ref, error_ref, groups, mean_buf, error_buf, mean_sem, error_sem = refs[2 * NX:]
    core, x = lax.axis_index("c"), lax.axis_index("x")
    p1, p2, p3 = split3(basis_ref[...])
    p_all = jnp.concatenate([p1, p1, p2, p2, p1, p3], axis=0).T
    copies = []
    for behind in range(NX):
        columns = pl.ds(pl.multiple_of((x - behind + NX) % NX * BLOCK, 128), BLOCK)
        for slot in range(SLOTS):
            groups[behind, z_at(core, slot, -1)] = own[behind][slot]
            groups[behind, z_at(1 - core, slot, -1)] = other[behind][slot]
        q_mean = jnp.concatenate([groups[behind, group] for group in range(NZ)], axis=0)
        mean_buf[behind] = q_mean
        copies.append(pltpu.make_async_copy(mean_buf.at[behind], mean_ref.at[:, columns], mean_sem.at[behind]))
        copies[-1].start()
        q1, q2, q3 = split3(q_mean)
        q_all = jnp.concatenate([q1, q2, q1, q2, q3, q1], axis=0)
        approx = jnp.dot(p_all, q_all, preferred_element_type=jnp.float32)
        error_buf[behind] = (merged_ref[:, columns].astype(jnp.float32) - approx).astype(jnp.bfloat16)
        copies.append(pltpu.make_async_copy(error_buf.at[behind], error_ref.at[0, :, columns], error_sem.at[behind]))
        copies[-1].start()
    for copy in copies:
        copy.wait()


def rewrite(own, other, basis, merged):
    return pl.pallas_call(
        rewrite_kernel,
        in_specs=[VMEM] * (2 * NX + 2),
        out_specs=[HBM, HBM],
        out_shape=[
            pltpu.HBM((R, COLS), jnp.float32),
            pltpu.HBM((1, ROWS, COLS), jnp.bfloat16),
        ],
        scratch_shapes=[
            pltpu.VMEM((NX, NZ, GROUP, BLOCK), jnp.float32),
            pltpu.VMEM((NX, R, BLOCK), jnp.float32),
            pltpu.VMEM((NX, ROWS, BLOCK), jnp.bfloat16),
            pltpu.SemaphoreType.DMA((NX,)),
            pltpu.SemaphoreType.DMA((NX,)),
        ],
        compiler_params=params(24),
        name="rewrite",
    )(*own, *other, basis, merged)


def shift(value, axis, size, by):
    return lax.ppermute(value, axis, [(i, (i + by) % size) for i in range(size)])


def swap(value, axis, size):
    return lax.ppermute(value, axis, [(i, i ^ 1) for i in range(size)])


def ring4(value, axis, size, unit):
    across = shift(value, axis, size, 2 * unit)
    left = shift(value, axis, size, unit)
    right = shift(value, axis, size, size - unit)
    return (value + across) + (left + right)


def z_round(value, slot):
    pairs = []
    for z in range(NZ):
        for core in range(NC):
            by = Z_SHIFTS[core][slot]
            if by != 0:
                pairs.append((z * NC + core, (z + by) % NZ * NC + core))
    return lax.ppermute(value, ("z", "c"), pairs)


def on_device(grads, error, q_in):
    merged, term = merge(grads, error, q_in.T)
    own = term + swap(term, "c", NC)
    own = ring4(own, "y", NY, 1)
    own = ring4(own, "x", NX, 1)
    mine = [z_round(own, slot) for slot in range(SLOTS)]
    theirs = [swap(value, "c", NC) for value in mine]
    basis, p_half = orthonormal(own, mine, theirs)

    half_shape, piece = (SLOTS, GROUP, BLOCK), (GROUP, BLOCK)
    keep, send = small(right_kernel, (NX,) + half_shape, 2, "right", p_half, merged,
                       scratch=[pltpu.VMEM((NX, NZ) + piece, jnp.float32)])
    own, one, two, three = small(chip_sum_kernel, half_shape, NX, "chip_sum", keep, swap(send, "c", NC))
    two = shift(two, "x", NX, 2)
    one = shift(one, "x", NX, 1)
    three = shift(three, "x", NX, 3)
    slots = small(x_sum_kernel, piece, SLOTS, "x_sum", own, one, two, three)
    got = [z_round(value, slot) for slot, value in enumerate(slots)]
    [part] = small(z_sum_kernel, piece, 1, "z_sum", slots[-1], *got)
    [mean] = small(mean_kernel, piece, 1, "mean", part, swap(part, "c", NC))

    got = [z_round(mean, slot) for slot in range(SLOTS)]
    [own] = small(collect_kernel, half_shape, 1, "collect", mean, *got)
    two = shift(own, "x", NX, 2)
    one = shift(own, "x", NX, 1)
    three = shift(own, "x", NX, 3)
    held = (own, one, two, three)
    q_mean, new_error = rewrite(held, [swap(value, "c", NC) for value in held], basis, merged)
    return basis.T, q_mean.T, new_error


def solution(mesh):
    fine = Mesh(mesh.devices.reshape(NX, NZ, NC, NY), ("x", "z", "c", "y"))
    replicas = ("x", "z", "c")
    in_specs = (P(replicas, None, "y"), P(replicas, None, "y"), P("y", None))
    out_specs = (P(), P("y", None), P(replicas, None, "y"))
    return jax.shard_map(
        on_device, mesh=fine, in_specs=in_specs, out_specs=out_specs, check_vma=False
    )
```

```python
import jax
import jax.numpy as jnp
from jax import lax
from jax.experimental import pallas as pl
from jax.experimental.pallas import tpu as pltpu
from jax.sharding import Mesh, PartitionSpec as P

EPS = 1e-06
NX, NZ, NC, NY = 4, 8, 2, 4
ROWS, R, COLS = 256, 32, 7168
GROUP = R // NZ
BLOCK = COLS // NX
HALF = R // NC
WIDTH = BLOCK // NC
PARTS = (NZ, GROUP, WIDTH)
REPLICAS = NX * NZ * NC

VMEM = pl.BlockSpec(memory_space=pltpu.VMEM)
HBM = pl.BlockSpec(memory_space=pltpu.HBM)
CHUNK = 512
CHUNKS = COLS // CHUNK


def params(mib):
    return pltpu.CompilerParams(vmem_limit_bytes=mib * 1024 * 1024)


def merge_kernel(grads_ref, error_ref, q_ref, merged_ref, keep_ref, send_ref, g_buf, e_buf, q_buf, g_sem, e_sem, q_sem):
    def copies(i):
        columns = pl.ds(i * CHUNK, CHUNK)
        return (
            pltpu.make_async_copy(grads_ref.at[0, :, columns], g_buf.at[i], g_sem.at[i]),
            pltpu.make_async_copy(error_ref.at[0, :, columns], e_buf.at[i], e_sem.at[i]),
            pltpu.make_async_copy(q_ref.at[:, columns], q_buf.at[i], q_sem.at[i]),
        )

    for i in range(CHUNKS):
        for copy in copies(i):
            copy.start()
    total = jnp.zeros((R, ROWS), jnp.float32)
    for i in range(CHUNKS):
        for copy in copies(i):
            copy.wait()
        merged = (g_buf[i].astype(jnp.float32) + e_buf[i].astype(jnp.float32)).astype(jnp.bfloat16)
        merged_ref[:, i * CHUNK:(i + 1) * CHUNK] = merged
        total += lax.dot_general(q_buf[i].astype(jnp.bfloat16), merged, (((1,), (1,)), ((), ())),
                                 preferred_element_type=jnp.float32)
    first = lax.axis_index("c") == 0
    low, high = total[:HALF], total[HALF:]
    keep_ref[...] = jnp.where(first, low, high)
    send_ref[...] = jnp.where(first, high, low)


def merge(grads, error, q_t):
    return pl.pallas_call(
        merge_kernel,
        in_specs=[HBM, HBM, HBM],
        out_specs=[VMEM, VMEM, VMEM],
        out_shape=[
            pltpu.VMEM((ROWS, COLS), jnp.bfloat16),
            pltpu.VMEM((HALF, ROWS), jnp.float32),
            pltpu.VMEM((HALF, ROWS), jnp.float32),
        ],
        scratch_shapes=[
            pltpu.VMEM((CHUNKS, ROWS, CHUNK), jnp.bfloat16),
            pltpu.VMEM((CHUNKS, ROWS, CHUNK), jnp.bfloat16),
            pltpu.VMEM((CHUNKS, R, CHUNK), jnp.float32),
            pltpu.SemaphoreType.DMA((CHUNKS,)),
            pltpu.SemaphoreType.DMA((CHUNKS,)),
            pltpu.SemaphoreType.DMA((CHUNKS,)),
        ],
        compiler_params=params(24),
        name="merge",
    )(*(pltpu.with_memory_space_constraint(a, pltpu.HBM) for a in (grads, error, q_t)))


def spread_kernel(keep_ref, got_ref, out_ref):
    total = keep_ref[...] + got_ref[...]
    for i in range(out_ref.shape[0]):
        out_ref[i] = total


def tree(terms):
    while len(terms) > 1:
        terms = [a + b for a, b in zip(terms[::2], terms[1::2])]
    return terms[0]


def spread_sum_kernel(terms_ref, out_ref):
    total = tree([terms_ref[i] for i in range(terms_ref.shape[0])])
    for i in range(out_ref.shape[0]):
        out_ref[i] = total


def sum_kernel(terms_ref, out_ref):
    out_ref[...] = tree([terms_ref[i] for i in range(terms_ref.shape[0])])


def orthonormal_kernel(own_ref, other_ref, basis_ref, half_ref):
    first = lax.axis_index("c") == 0
    own, other = own_ref[...], other_ref[...]
    total = jnp.concatenate([jnp.where(first, own, other), jnp.where(first, other, own)], axis=0)
    tiles = [total[8 * i:8 * i + 8] for i in range(R // 8)]
    left = list(tiles)
    basis = [jnp.zeros_like(tile) for tile in tiles]
    rows = lax.broadcasted_iota(jnp.int32, (8, 1), 0)
    for column in range(R):
        tile, row = divmod(column, 8)
        vector = left[tile][row:row + 1]
        if column > 0:
            built = (column - 1) // 8 + 1
            taken = None
            for part in basis[:built]:
                term = jnp.sum(part * vector, axis=1, keepdims=True) * part
                taken = term if taken is None else taken + term
            vector = vector - jnp.sum(taken, axis=0, keepdims=True)
        products = [jnp.sum(tiles[later] * vector, axis=1, keepdims=True) for later in range((column + 1) // 8, R // 8)]
        scale = lax.rsqrt(jnp.sum(vector * vector, axis=1, keepdims=True) + EPS)
        basis[tile] = jnp.where(rows == row, vector * scale, basis[tile])
        square = scale * scale
        for later, product in zip(range((column + 1) // 8, R // 8), products):
            left[later] = left[later] - (product * square) * vector
    result = jnp.concatenate(basis, axis=0)
    basis_ref[...] = result
    half_ref[...] = result.astype(jnp.bfloat16)


def small(kernel, out, count, name, *args, scratch=()):
    return pl.pallas_call(
        kernel,
        in_specs=[VMEM] * len(args),
        out_specs=[VMEM] * count,
        out_shape=[pltpu.VMEM(out, jnp.float32)] * count,
        scratch_shapes=list(scratch),
        compiler_params=params(16),
        name=name,
    )(*args)


def orthonormal(own, other):
    return pl.pallas_call(
        orthonormal_kernel,
        in_specs=[VMEM, VMEM],
        out_specs=[VMEM, VMEM],
        out_shape=[
            pltpu.VMEM((R, ROWS), jnp.float32),
            pltpu.VMEM((R, ROWS), jnp.bfloat16),
        ],
        compiler_params=params(16),
        name="orthonormal",
    )(own, other)


def right_kernel(half_ref, merged_ref, keep_ref, send_ref, groups):
    half = half_ref[...]
    core, x = lax.axis_index("c"), lax.axis_index("x")
    for block in range(NX):
        term = jnp.dot(half, merged_ref[:, block * BLOCK:(block + 1) * BLOCK], preferred_element_type=jnp.float32)
        for owner in range(NC):
            for group in range(NZ):
                groups[block, owner, group] = term[group * GROUP:(group + 1) * GROUP, owner * WIDTH:(owner + 1) * WIDTH]
    for ahead in range(NX):
        block = (x + ahead) % NX
        keep_ref[ahead] = groups[block, core]
        send_ref[ahead] = groups[block, 1 - core]


def chip_sum_kernel(keep_ref, got_ref, *outs):
    for ahead, out in enumerate(outs):
        out[...] = keep_ref[ahead] + got_ref[ahead]


def x_sum_kernel(two_ref, one_ref, three_ref, own_ref, out_ref):
    out_ref[...] = (own_ref[...] + two_ref[...]) + (one_ref[...] + three_ref[...])


def mean_kernel(terms_ref, out_ref):
    total = tree([terms_ref[i] for i in range(NZ)]) * (1.0 / REPLICAS)
    for i in range(NZ):
        out_ref[i] = total


def split3(value):
    first = value.astype(jnp.bfloat16)
    rest = value - first.astype(jnp.float32)
    second = rest.astype(jnp.bfloat16)
    third = (rest - second.astype(jnp.float32)).astype(jnp.bfloat16)
    return first, second, third


def left_kernel(basis_ref, left_ref):
    p1, p2, p3 = split3(basis_ref[...])
    left_ref[...] = jnp.concatenate([p1, p1, p2, p2, p1, p3], axis=0).T


def left_factor(basis):
    return pl.pallas_call(
        left_kernel,
        in_specs=[VMEM],
        out_specs=VMEM,
        out_shape=pltpu.VMEM((ROWS, 6 * R), jnp.bfloat16),
        compiler_params=params(16),
        name="left_factor",
    )(basis)


def rewrite(places, values, left, merged, so_far):
    count = len(values)

    def kernel(*refs):
        held, (left_ref, merged_ref) = refs[:count], refs[count:count + 2]
        mean_ref, error_ref, mean_buf, error_buf, mean_sem, error_sem = refs[-6:]
        core, x = lax.axis_index("c"), lax.axis_index("x")
        copies = []
        for i, (behind, away) in enumerate(places):
            owner = 1 - core if away else core
            start = (x - behind + NX) % NX * BLOCK + owner * WIDTH
            columns = pl.ds(pl.multiple_of(start, 128), WIDTH)
            q_mean = jnp.concatenate([held[i][group] for group in range(NZ)], axis=0)
            mean_buf[i] = q_mean
            copies.append(pltpu.make_async_copy(mean_buf.at[i], mean_ref.at[:, columns], mean_sem.at[i]))
            copies[-1].start()
            q1, q2, q3 = split3(q_mean)
            q_all = jnp.concatenate([q1, q2, q1, q2, q3, q1], axis=0)
            approx = jnp.dot(left_ref[...], q_all, preferred_element_type=jnp.float32)
            error_buf[i] = (merged_ref[:, columns].astype(jnp.float32) - approx).astype(jnp.bfloat16)
            copies.append(pltpu.make_async_copy(error_buf.at[i], error_ref.at[0, :, columns], error_sem.at[i]))
            copies[-1].start()
        for copy in copies:
            copy.wait()

    return pl.pallas_call(
        kernel,
        in_specs=[VMEM] * (count + 2) + [HBM] * len(so_far),
        out_specs=[HBM, HBM],
        out_shape=[
            pltpu.HBM((R, COLS), jnp.float32),
            pltpu.HBM((1, ROWS, COLS), jnp.bfloat16),
        ],
        scratch_shapes=[
            pltpu.VMEM((count, R, WIDTH), jnp.float32),
            pltpu.VMEM((count, ROWS, WIDTH), jnp.bfloat16),
            pltpu.SemaphoreType.DMA((count,)),
            pltpu.SemaphoreType.DMA((count,)),
        ],
        input_output_aliases={count + 2 + i: i for i in range(len(so_far))},
        cost_estimate=pl.CostEstimate(flops=2 * count * ROWS * 6 * R * WIDTH, transcendentals=0,
                                      bytes_accessed=4 * count * (ROWS + R) * WIDTH),
        compiler_params=params(16),
        name="rewrite",
    )(*values, left, merged, *so_far)


def shift(value, axis, size, by):
    return lax.ppermute(value, axis, [(i, (i + by) % size) for i in range(size)])


def swap(value, axis, size):
    return lax.ppermute(value, axis, [(i, i ^ 1) for i in range(size)])


def exchange(value, axes):
    return lax.all_to_all(value, axes, 0, 0, tiled=True)


def x_ring(two, one, three):
    return shift(two, "x", NX, 2), shift(one, "x", NX, 1), shift(three, "x", NX, 3)


def on_device(grads, error, q_in):
    merged, keep, send = merge(grads, error, q_in.T)
    [terms] = small(spread_kernel, (NX * NY, HALF, ROWS), 1, "spread", keep, swap(send, "c", NC))
    [terms] = small(spread_sum_kernel, (NZ, HALF, ROWS), 1, "spread_sum", exchange(terms, ("x", "y")))
    [own] = small(sum_kernel, (HALF, ROWS), 1, "sum", exchange(terms, "z"))
    basis, p_half = orthonormal(own, swap(own, "c", NC))

    keep, send = small(right_kernel, (NX,) + PARTS, 2, "right", p_half, merged,
                       scratch=[pltpu.VMEM((NX, NC) + PARTS, jnp.float32)])
    own, one, two, three = small(chip_sum_kernel, PARTS, NX, "chip_sum", keep, swap(send, "c", NC))
    [own] = small(x_sum_kernel, PARTS, 1, "x_sum", *x_ring(two, one, three), own)
    [mean] = small(mean_kernel, PARTS, 1, "mean", exchange(own, "z"))
    own = exchange(mean, "z")

    two, one, three = x_ring(own, own, own)
    left = left_factor(basis)
    done = rewrite([(0, 0), (0, 1)], [own, swap(own, "c", NC)], left, merged, [])
    one, three, two, done = lax.optimization_barrier((one, three, two, done))
    far = [swap(value, "c", NC) for value in (one, three, two)]
    done = rewrite([(1, 0), (3, 0), (2, 0)], [one, three, two], left, merged, done)
    q_mean, new_error = rewrite([(1, 1), (3, 1), (2, 1)], far, left, merged, done)
    return basis.T, q_mean.T, new_error


def solution(mesh):
    fine = Mesh(mesh.devices.reshape(NX, NZ, NC, NY), ("x", "z", "c", "y"))
    replicas = ("x", "z", "c")
    in_specs = (P(replicas, None, "y"), P(replicas, None, "y"), P("y", None))
    out_specs = (P(), P("y", None), P(replicas, None, "y"))
    return jax.shard_map(
        on_device, mesh=fine, in_specs=in_specs, out_specs=out_specs, check_vma=False
    )
```

```python
import jax
import jax.numpy as jnp
from jax import lax
from jax.experimental import pallas as pl
from jax.experimental.pallas import tpu as pltpu
from jax.sharding import Mesh, PartitionSpec as P

EPS = 1e-06
NX, NZ, NC, NY = 4, 8, 2, 4
ROWS, R, COLS = 256, 32, 7168
GROUP = R // NZ
BLOCK = COLS // NX
HALF = R // NC
WIDTH = BLOCK // NC
PARTS = (NZ, GROUP, WIDTH)
REPLICAS = NX * NZ * NC

VMEM = pl.BlockSpec(memory_space=pltpu.VMEM)
HBM = pl.BlockSpec(memory_space=pltpu.HBM)
CHUNK = 512
CHUNKS = COLS // CHUNK


def params(mib):
    return pltpu.CompilerParams(vmem_limit_bytes=mib * 1024 * 1024)


def merge_kernel(grads_ref, error_ref, q_ref, merged_ref, keep_ref, send_ref, g_buf, e_buf, q_buf, g_sem, e_sem, q_sem):
    def copies(i):
        columns = pl.ds(i * CHUNK, CHUNK)
        return (
            pltpu.make_async_copy(grads_ref.at[0, :, columns], g_buf.at[i], g_sem.at[i]),
            pltpu.make_async_copy(error_ref.at[0, :, columns], e_buf.at[i], e_sem.at[i]),
            pltpu.make_async_copy(q_ref.at[:, columns], q_buf.at[i], q_sem.at[i]),
        )

    for i in range(CHUNKS):
        for copy in copies(i):
            copy.start()
    total = jnp.zeros((R, ROWS), jnp.float32)
    for i in range(CHUNKS):
        for copy in copies(i):
            copy.wait()
        merged = (g_buf[i].astype(jnp.float32) + e_buf[i].astype(jnp.float32)).astype(jnp.bfloat16)
        merged_ref[:, i * CHUNK:(i + 1) * CHUNK] = merged
        total += lax.dot_general(q_buf[i].astype(jnp.bfloat16), merged, (((1,), (1,)), ((), ())),
                                 preferred_element_type=jnp.float32)
    first = lax.axis_index("c") == 0
    low, high = total[:HALF], total[HALF:]
    keep_ref[...] = jnp.where(first, low, high)
    send_ref[...] = jnp.where(first, high, low)


def merge(grads, error, q_t):
    return pl.pallas_call(
        merge_kernel,
        in_specs=[HBM, HBM, HBM],
        out_specs=[VMEM, VMEM, VMEM],
        out_shape=[
            pltpu.VMEM((ROWS, COLS), jnp.bfloat16),
            pltpu.VMEM((HALF, ROWS), jnp.float32),
            pltpu.VMEM((HALF, ROWS), jnp.float32),
        ],
        scratch_shapes=[
            pltpu.VMEM((CHUNKS, ROWS, CHUNK), jnp.bfloat16),
            pltpu.VMEM((CHUNKS, ROWS, CHUNK), jnp.bfloat16),
            pltpu.VMEM((CHUNKS, R, CHUNK), jnp.float32),
            pltpu.SemaphoreType.DMA((CHUNKS,)),
            pltpu.SemaphoreType.DMA((CHUNKS,)),
            pltpu.SemaphoreType.DMA((CHUNKS,)),
        ],
        compiler_params=params(24),
        name="merge",
    )(*(pltpu.with_memory_space_constraint(a, pltpu.HBM) for a in (grads, error, q_t)))


def spread_kernel(keep_ref, got_ref, out_ref):
    total = keep_ref[...] + got_ref[...]
    for i in range(out_ref.shape[0]):
        out_ref[i] = total


def tree(terms):
    while len(terms) > 1:
        terms = [a + b for a, b in zip(terms[::2], terms[1::2])]
    return terms[0]


def spread_sum_kernel(terms_ref, out_ref):
    total = tree([terms_ref[i] for i in range(terms_ref.shape[0])])
    for i in range(out_ref.shape[0]):
        out_ref[i] = total


def sum_kernel(terms_ref, out_ref):
    out_ref[...] = tree([terms_ref[i] for i in range(terms_ref.shape[0])])


def orthonormal_kernel(own_ref, other_ref, basis_ref, half_ref):
    first = lax.axis_index("c") == 0
    own, other = own_ref[...], other_ref[...]
    total = jnp.concatenate([jnp.where(first, own, other), jnp.where(first, other, own)], axis=0)
    tiles = [total[8 * i:8 * i + 8] for i in range(R // 8)]
    left = list(tiles)
    basis = [jnp.zeros_like(tile) for tile in tiles]
    rows = lax.broadcasted_iota(jnp.int32, (8, 1), 0)
    for column in range(R):
        tile, row = divmod(column, 8)
        vector = left[tile][row:row + 1]
        if column > 0:
            built = (column - 1) // 8 + 1
            taken = None
            for part in basis[:built]:
                term = jnp.sum(part * vector, axis=1, keepdims=True) * part
                taken = term if taken is None else taken + term
            vector = vector - jnp.sum(taken, axis=0, keepdims=True)
        products = [jnp.sum(tiles[later] * vector, axis=1, keepdims=True) for later in range((column + 1) // 8, R // 8)]
        scale = lax.rsqrt(jnp.sum(vector * vector, axis=1, keepdims=True) + EPS)
        basis[tile] = jnp.where(rows == row, vector * scale, basis[tile])
        square = scale * scale
        for later, product in zip(range((column + 1) // 8, R // 8), products):
            left[later] = left[later] - (product * square) * vector
    result = jnp.concatenate(basis, axis=0)
    basis_ref[...] = result
    half_ref[...] = result.astype(jnp.bfloat16)


def small(kernel, out, count, name, *args, scratch=()):
    return pl.pallas_call(
        kernel,
        in_specs=[VMEM] * len(args),
        out_specs=[VMEM] * count,
        out_shape=[pltpu.VMEM(out, jnp.float32)] * count,
        scratch_shapes=list(scratch),
        compiler_params=params(16),
        name=name,
    )(*args)


def orthonormal(own, other):
    return pl.pallas_call(
        orthonormal_kernel,
        in_specs=[VMEM, VMEM],
        out_specs=[VMEM, VMEM],
        out_shape=[
            pltpu.VMEM((R, ROWS), jnp.float32),
            pltpu.VMEM((R, ROWS), jnp.bfloat16),
        ],
        compiler_params=params(16),
        name="orthonormal",
    )(own, other)


def right(p_half, merged, blocks_ahead):
    count = len(blocks_ahead)

    def kernel(half_ref, merged_ref, keep_ref, send_ref, groups):
        core, x = lax.axis_index("c"), lax.axis_index("x")
        for i, ahead in enumerate(blocks_ahead):
            columns = pl.ds(pl.multiple_of((x + ahead) % NX * BLOCK, 128), BLOCK)
            term = jnp.dot(half_ref[...], merged_ref[:, columns], preferred_element_type=jnp.float32)
            for owner in range(NC):
                for group in range(NZ):
                    groups[i, owner, group] = term[group * GROUP:(group + 1) * GROUP, owner * WIDTH:(owner + 1) * WIDTH]
            keep_ref[i] = groups[i, core]
            send_ref[i] = groups[i, 1 - core]

    return small(kernel, (count,) + PARTS, 2, "right", p_half, merged,
                 scratch=[pltpu.VMEM((count, NC) + PARTS, jnp.float32)])


def chip_sum_kernel(keep_ref, got_ref, *outs):
    for i, out in enumerate(outs):
        out[...] = keep_ref[i] + got_ref[i]


def x_sum_kernel(two_ref, one_ref, three_ref, own_ref, out_ref):
    out_ref[...] = (own_ref[...] + two_ref[...]) + (one_ref[...] + three_ref[...])


def mean_kernel(terms_ref, out_ref):
    total = tree([terms_ref[i] for i in range(NZ)]) * (1.0 / REPLICAS)
    for i in range(NZ):
        out_ref[i] = total


def split3(value):
    first = value.astype(jnp.bfloat16)
    rest = value - first.astype(jnp.float32)
    second = rest.astype(jnp.bfloat16)
    third = (rest - second.astype(jnp.float32)).astype(jnp.bfloat16)
    return first, second, third


def left_kernel(basis_ref, left_ref):
    p1, p2, p3 = split3(basis_ref[...])
    left_ref[...] = jnp.concatenate([p1, p1, p2, p2, p1, p3], axis=0).T


def left_factor(basis):
    return pl.pallas_call(
        left_kernel,
        in_specs=[VMEM],
        out_specs=VMEM,
        out_shape=pltpu.VMEM((ROWS, 6 * R), jnp.bfloat16),
        compiler_params=params(16),
        name="left_factor",
    )(basis)


def columns_of(place):
    behind, away = place
    core, x = lax.axis_index("c"), lax.axis_index("x")
    start = (x - behind + NX) % NX * BLOCK + (1 - core if away else core) * WIDTH
    return pl.ds(pl.multiple_of(start, 128), WIDTH)


def rewrite(places, values, left, merged, before=(), pending=(), done=(), last=False):
    count, waiting = len(values), len(pending)
    leaves = not last
    writes = bool(before) or last

    def kernel(*refs):
        refs = list(refs)

        def take(n):
            taken, refs[:n] = refs[:n], []
            return taken

        held, (left_ref, merged_ref), late = take(count), take(2), take(waiting)
        take(len(done))
        out = take(2) if writes else None
        mean_refs, error_refs = take(count), take(count)
        sems = refs[0] if writes else None
        copies = []

        def write(place, mean, error):
            columns = columns_of(place)
            for source, target in ((mean, out[0].at[:, columns]), (error, out[1].at[0, :, columns])):
                copies.append(pltpu.make_async_copy(source, target, sems.at[len(copies)]))
                copies[-1].start()

        for i, place in enumerate(before):
            write(place, late[i], late[len(before) + i])
        for i, place in enumerate(places):
            q_mean = jnp.concatenate([held[i][group] for group in range(NZ)], axis=0)
            mean_refs[i][...] = q_mean
            q1, q2, q3 = split3(q_mean)
            q_all = jnp.concatenate([q1, q2, q1, q2, q3, q1], axis=0)
            approx = jnp.dot(left_ref[...], q_all, preferred_element_type=jnp.float32)
            error_refs[i][...] = (merged_ref[:, columns_of(place)].astype(jnp.float32) - approx).astype(jnp.bfloat16)
            if last:
                write(place, mean_refs[i], error_refs[i])
        for copy in copies:
            copy.wait()

    results = [pltpu.HBM((R, COLS), jnp.float32), pltpu.HBM((1, ROWS, COLS), jnp.bfloat16)] if writes else []
    parts = [pltpu.VMEM((R, WIDTH), jnp.float32)] * count + [pltpu.VMEM((ROWS, WIDTH), jnp.bfloat16)] * count
    copies = 2 * (len(before) + (count if last else 0))
    outs = pl.pallas_call(
        kernel,
        in_specs=[VMEM] * (count + 2 + waiting) + [HBM] * len(done),
        out_specs=[HBM] * len(results) + ([VMEM] * len(parts) if leaves else []),
        out_shape=results + (parts if leaves else []),
        scratch_shapes=([] if leaves else parts) + ([pltpu.SemaphoreType.DMA((copies,))] if copies else []),
        input_output_aliases={count + 2 + waiting + i: i for i in range(len(done))},
        cost_estimate=pl.CostEstimate(flops=2 * count * ROWS * 6 * R * WIDTH, transcendentals=0,
                                      bytes_accessed=4 * count * (ROWS + R) * WIDTH),
        compiler_params=params(16),
        name="rewrite",
    )(*values, left, merged, *pending, *done)
    return outs[:len(results)], outs[len(results):]


def shift(value, axis, size, by):
    return lax.ppermute(value, axis, [(i, (i + by) % size) for i in range(size)])


def swap(value, axis, size):
    return lax.ppermute(value, axis, [(i, i ^ 1) for i in range(size)])


def exchange(value, axes):
    return lax.all_to_all(value, axes, 0, 0, tiled=True)


def x_ring(two, one, three):
    return shift(two, "x", NX, 2), shift(one, "x", NX, 1), shift(three, "x", NX, 3)


def on_device(grads, error, q_in):
    merged, keep, send = merge(grads, error, q_in.T)
    [terms] = small(spread_kernel, (NX * NY, HALF, ROWS), 1, "spread", keep, swap(send, "c", NC))
    [terms] = small(spread_sum_kernel, (NZ, HALF, ROWS), 1, "spread_sum", exchange(terms, ("x", "y")))
    [own] = small(sum_kernel, (HALF, ROWS), 1, "sum", exchange(terms, "z"))
    basis, p_half = orthonormal(own, swap(own, "c", NC))

    keep, send = right(p_half, merged, range(NX))
    own, one, two, three = small(chip_sum_kernel, PARTS, NX, "chip_sum", keep, swap(send, "c", NC))
    [own] = small(x_sum_kernel, PARTS, 1, "x_sum", *x_ring(two, one, three), own)
    [mean] = small(mean_kernel, PARTS, 1, "mean", exchange(own, "z"))
    own = exchange(mean, "z")

    two, one, three = x_ring(own, own, own)
    left = left_factor(basis)
    places = [(0, 0), (0, 1)]
    _, pending = rewrite(places, [own, swap(own, "c", NC)], left, merged)
    two, *pending = lax.optimization_barrier((two, *pending))
    far_two = swap(two, "c", NC)
    done, pending = rewrite([(2, 0)], [two], left, merged, places, pending)
    three, one, *pending = lax.optimization_barrier((three, one, *pending))
    far_three, far_one = swap(three, "c", NC), swap(one, "c", NC)
    places = [(3, 0), (1, 0), (2, 1)]
    done, pending = rewrite(places, [three, one, far_two], left, merged, [(2, 0)], pending, done)
    (q_mean, new_error), _ = rewrite([(3, 1), (1, 1)], [far_three, far_one], left, merged, places, pending, done, last=True)
    return basis.T, q_mean.T, new_error


def solution(mesh):
    fine = Mesh(mesh.devices.reshape(NX, NZ, NC, NY), ("x", "z", "c", "y"))
    replicas = ("x", "z", "c")
    in_specs = (P(replicas, None, "y"), P(replicas, None, "y"), P("y", None))
    out_specs = (P(), P("y", None), P(replicas, None, "y"))
    return jax.shard_map(
        on_device, mesh=fine, in_specs=in_specs, out_specs=out_specs, check_vma=False
    )
```

```python
import jax
import jax.numpy as jnp
from jax import lax
from jax.experimental import pallas as pl
from jax.experimental.pallas import tpu as pltpu
from jax.sharding import Mesh, PartitionSpec as P

EPS = 1e-06
NX, NZ, NC, NY = 4, 8, 2, 4
ROWS, R, COLS = 256, 32, 7168
GROUP = R // NZ
BLOCK = COLS // NX
SLOTS = NZ // NC
WIDTH = BLOCK // NC
PARTS = (NZ, GROUP, WIDTH)
REPLICAS = NX * NZ * NC

VMEM = pl.BlockSpec(memory_space=pltpu.VMEM)
HBM = pl.BlockSpec(memory_space=pltpu.HBM)
CHUNK = 512
CHUNKS = COLS // CHUNK
Z_SHIFTS = ((4, 3, 1, 0), (-3, 2, -2, -1))


def params(mib):
    return pltpu.CompilerParams(vmem_limit_bytes=mib * 1024 * 1024)


def merge_kernel(grads_ref, error_ref, q_ref, merged_ref, term_ref, g_buf, e_buf, q_buf, g_sem, e_sem, q_sem):
    def copies(i):
        columns = pl.ds(i * CHUNK, CHUNK)
        return (
            pltpu.make_async_copy(grads_ref.at[0, :, columns], g_buf.at[i], g_sem.at[i]),
            pltpu.make_async_copy(error_ref.at[0, :, columns], e_buf.at[i], e_sem.at[i]),
            pltpu.make_async_copy(q_ref.at[:, columns], q_buf.at[i], q_sem.at[i]),
        )

    for i in range(CHUNKS):
        for copy in copies(i):
            copy.start()
    total = jnp.zeros((R, ROWS), jnp.float32)
    for i in range(CHUNKS):
        for copy in copies(i):
            copy.wait()
        merged = (g_buf[i].astype(jnp.float32) + e_buf[i].astype(jnp.float32)).astype(jnp.bfloat16)
        merged_ref[:, i * CHUNK:(i + 1) * CHUNK] = merged
        total += lax.dot_general(q_buf[i].astype(jnp.bfloat16), merged, (((1,), (1,)), ((), ())),
                                 preferred_element_type=jnp.float32)
    term_ref[...] = total


def merge(grads, error, q_t):
    return pl.pallas_call(
        merge_kernel,
        in_specs=[HBM, HBM, HBM],
        out_specs=[VMEM, VMEM],
        out_shape=[
            pltpu.VMEM((ROWS, COLS), jnp.bfloat16),
            pltpu.VMEM((R, ROWS), jnp.float32),
        ],
        scratch_shapes=[
            pltpu.VMEM((CHUNKS, ROWS, CHUNK), jnp.bfloat16),
            pltpu.VMEM((CHUNKS, ROWS, CHUNK), jnp.bfloat16),
            pltpu.VMEM((CHUNKS, R, CHUNK), jnp.float32),
            pltpu.SemaphoreType.DMA((CHUNKS,)),
            pltpu.SemaphoreType.DMA((CHUNKS,)),
            pltpu.SemaphoreType.DMA((CHUNKS,)),
        ],
        compiler_params=params(24),
        name="merge",
    )(*(pltpu.with_memory_space_constraint(a, pltpu.HBM) for a in (grads, error, q_t)))


def tree(terms):
    while len(terms) > 1:
        terms = [a + b for a, b in zip(terms[::2], terms[1::2])]
    return terms[0]


def z_at(core, slot, sign):
    low, high = Z_SHIFTS[0][slot], Z_SHIFTS[1][slot]
    return (lax.axis_index("z") + jnp.where(core == 0, sign * low, sign * high) + NZ) % NZ


def orthonormal_kernel(own_ref, *refs):
    mine, theirs = refs[:SLOTS], refs[SLOTS:2 * SLOTS]
    basis_ref, half_ref, ring = refs[2 * SLOTS:]
    core = lax.axis_index("c")
    for group, owner in ((mine, core), (theirs, 1 - core)):
        for slot, ref in enumerate(group):
            ring[z_at(owner, slot, -1)] = ref[...]
    ring[lax.axis_index("z")] = own_ref[...]
    total = (ring[0] + ring[1]) + (ring[2] + ring[3])
    total = total + ((ring[4] + ring[5]) + (ring[6] + ring[7]))

    tiles = [total[8 * i:8 * i + 8] for i in range(R // 8)]
    left = list(tiles)
    basis = [jnp.zeros_like(tile) for tile in tiles]
    rows = lax.broadcasted_iota(jnp.int32, (8, 1), 0)
    for column in range(R):
        tile, row = divmod(column, 8)
        vector = left[tile][row:row + 1]
        if column > 0:
            built = (column - 1) // 8 + 1
            taken = None
            for part in basis[:built]:
                term = jnp.sum(part * vector, axis=1, keepdims=True) * part
                taken = term if taken is None else taken + term
            vector = vector - jnp.sum(taken, axis=0, keepdims=True)
        products = [jnp.sum(tiles[later] * vector, axis=1, keepdims=True) for later in range((column + 1) // 8, R // 8)]
        scale = lax.rsqrt(jnp.sum(vector * vector, axis=1, keepdims=True) + EPS)
        basis[tile] = jnp.where(rows == row, vector * scale, basis[tile])
        square = scale * scale
        for later, product in zip(range((column + 1) // 8, R // 8), products):
            left[later] = left[later] - (product * square) * vector
    result = jnp.concatenate(basis, axis=0)
    basis_ref[...] = result
    half_ref[...] = result.astype(jnp.bfloat16)


def small(kernel, out, count, name, *args, scratch=()):
    return pl.pallas_call(
        kernel,
        in_specs=[VMEM] * len(args),
        out_specs=[VMEM] * count,
        out_shape=[pltpu.VMEM(out, jnp.float32)] * count,
        scratch_shapes=list(scratch),
        compiler_params=params(16),
        name=name,
    )(*args)


def orthonormal(own, mine, theirs):
    return pl.pallas_call(
        orthonormal_kernel,
        in_specs=[VMEM] * (1 + 2 * SLOTS),
        out_specs=[VMEM, VMEM],
        out_shape=[
            pltpu.VMEM((R, ROWS), jnp.float32),
            pltpu.VMEM((R, ROWS), jnp.bfloat16),
        ],
        scratch_shapes=[pltpu.VMEM((NZ, R, ROWS), jnp.float32)],
        compiler_params=params(16),
        name="orthonormal",
    )(own, *mine, *theirs)


def right(p_half, merged, blocks_ahead):
    count = len(blocks_ahead)

    def kernel(half_ref, merged_ref, keep_ref, send_ref, groups):
        core, x = lax.axis_index("c"), lax.axis_index("x")
        for i, ahead in enumerate(blocks_ahead):
            columns = pl.ds(pl.multiple_of((x + ahead) % NX * BLOCK, 128), BLOCK)
            term = jnp.dot(half_ref[...], merged_ref[:, columns], preferred_element_type=jnp.float32)
            for owner in range(NC):
                for group in range(NZ):
                    groups[i, owner, group] = term[group * GROUP:(group + 1) * GROUP, owner * WIDTH:(owner + 1) * WIDTH]
            keep_ref[i] = groups[i, core]
            send_ref[i] = groups[i, 1 - core]

    return small(kernel, (count,) + PARTS, 2, "right", p_half, merged,
                 scratch=[pltpu.VMEM((count, NC) + PARTS, jnp.float32)])


def chip_sum_kernel(keep_ref, got_ref, *outs):
    for i, out in enumerate(outs):
        out[...] = keep_ref[i] + got_ref[i]


def x_sum_kernel(two_ref, one_ref, three_ref, own_ref, out_ref):
    out_ref[...] = (own_ref[...] + two_ref[...]) + (one_ref[...] + three_ref[...])


def mean_kernel(terms_ref, out_ref):
    total = tree([terms_ref[i] for i in range(NZ)]) * (1.0 / REPLICAS)
    for i in range(NZ):
        out_ref[i] = total


def split3(value):
    first = value.astype(jnp.bfloat16)
    rest = value - first.astype(jnp.float32)
    second = rest.astype(jnp.bfloat16)
    third = (rest - second.astype(jnp.float32)).astype(jnp.bfloat16)
    return first, second, third


def left_kernel(basis_ref, left_ref, out_ref, sem):
    copy = pltpu.make_async_copy(basis_ref, out_ref, sem)
    copy.start()
    p1, p2, p3 = split3(basis_ref[...])
    left_ref[...] = jnp.concatenate([p1, p1, p2, p2, p1, p3], axis=0).T
    copy.wait()


def left_factor(basis):
    return pl.pallas_call(
        left_kernel,
        in_specs=[VMEM],
        out_specs=[VMEM, HBM],
        out_shape=[pltpu.VMEM((ROWS, 6 * R), jnp.bfloat16), pltpu.HBM((R, ROWS), jnp.float32)],
        scratch_shapes=[pltpu.SemaphoreType.DMA],
        compiler_params=params(16),
        name="left_factor",
    )(basis)


def rewrite(places, values, left, merged, so_far):
    count = len(values)

    def kernel(*refs):
        held, (left_ref, merged_ref) = refs[:count], refs[count:count + 2]
        mean_ref, error_ref, mean_buf, error_buf, mean_sem, error_sem = refs[-6:]
        core, x = lax.axis_index("c"), lax.axis_index("x")
        copies = []
        for i, (behind, away) in enumerate(places):
            owner = 1 - core if away else core
            start = (x - behind + NX) % NX * BLOCK + owner * WIDTH
            columns = pl.ds(pl.multiple_of(start, 128), WIDTH)
            q_mean = jnp.concatenate([held[i][group] for group in range(NZ)], axis=0)
            mean_buf[i] = q_mean
            copies.append(pltpu.make_async_copy(mean_buf.at[i], mean_ref.at[:, columns], mean_sem.at[i]))
            copies[-1].start()
            q1, q2, q3 = split3(q_mean)
            q_all = jnp.concatenate([q1, q2, q1, q2, q3, q1], axis=0)
            approx = jnp.dot(left_ref[...], q_all, preferred_element_type=jnp.float32)
            error_buf[i] = (merged_ref[:, columns].astype(jnp.float32) - approx).astype(jnp.bfloat16)
            copies.append(pltpu.make_async_copy(error_buf.at[i], error_ref.at[0, :, columns], error_sem.at[i]))
            copies[-1].start()
        for copy in copies:
            copy.wait()

    return pl.pallas_call(
        kernel,
        in_specs=[VMEM] * (count + 2) + [HBM] * len(so_far),
        out_specs=[HBM, HBM],
        out_shape=[
            pltpu.HBM((R, COLS), jnp.float32),
            pltpu.HBM((1, ROWS, COLS), jnp.bfloat16),
        ],
        scratch_shapes=[
            pltpu.VMEM((count, R, WIDTH), jnp.float32),
            pltpu.VMEM((count, ROWS, WIDTH), jnp.bfloat16),
            pltpu.SemaphoreType.DMA((count,)),
            pltpu.SemaphoreType.DMA((count,)),
        ],
        input_output_aliases={count + 2 + i: i for i in range(len(so_far))},
        cost_estimate=pl.CostEstimate(flops=2 * count * ROWS * 6 * R * WIDTH, transcendentals=0,
                                      bytes_accessed=4 * count * (ROWS + R) * WIDTH),
        compiler_params=params(16),
        name="rewrite",
    )(*values, left, merged, *so_far)


def shift(value, axis, size, by):
    return lax.ppermute(value, axis, [(i, (i + by) % size) for i in range(size)])


def swap(value, axis, size):
    return lax.ppermute(value, axis, [(i, i ^ 1) for i in range(size)])


def ring4(value, axis, size, unit):
    across = shift(value, axis, size, 2 * unit)
    left = shift(value, axis, size, unit)
    right = shift(value, axis, size, size - unit)
    return (value + across) + (left + right)


def z_round(value, slot):
    pairs = []
    for z in range(NZ):
        for core in range(NC):
            by = Z_SHIFTS[core][slot]
            if by != 0:
                pairs.append((z * NC + core, (z + by) % NZ * NC + core))
    return lax.ppermute(value, ("z", "c"), pairs)


def exchange(value, axes):
    return lax.all_to_all(value, axes, 0, 0, tiled=True)


def x_ring(two, one, three):
    return shift(two, "x", NX, 2), shift(one, "x", NX, 1), shift(three, "x", NX, 3)


def on_device(grads, error, q_in):
    merged, term = merge(grads, error, q_in.T)
    own = term + swap(term, "c", NC)
    own = ring4(own, "y", NY, 1)
    own = ring4(own, "x", NX, 1)
    mine = [z_round(own, slot) for slot in range(SLOTS)]
    theirs = [swap(value, "c", NC) for value in mine]
    basis, p_half = orthonormal(own, mine, theirs)

    keep, send = right(p_half, merged, range(NX))
    own, one, two, three = small(chip_sum_kernel, PARTS, NX, "chip_sum", keep, swap(send, "c", NC))
    [own] = small(x_sum_kernel, PARTS, 1, "x_sum", *x_ring(two, one, three), own)
    [mean] = small(mean_kernel, PARTS, 1, "mean", exchange(own, "z"))
    own = exchange(mean, "z")

    two, one, three = x_ring(own, own, own)
    left, p_basis = left_factor(basis)
    done = rewrite([(0, 0), (0, 1)], [own, swap(own, "c", NC)], left, merged, [])
    two, *done = lax.optimization_barrier((two, *done))
    far_two = swap(two, "c", NC)
    done = rewrite([(2, 0)], [two], left, merged, done)
    three, one, *done = lax.optimization_barrier((three, one, *done))
    far_three, far_one = swap(three, "c", NC), swap(one, "c", NC)
    done = rewrite([(3, 0), (1, 0), (2, 1)], [three, one, far_two], left, merged, done)
    q_mean, new_error = rewrite([(3, 1), (1, 1)], [far_three, far_one], left, merged, done)
    return p_basis.T, q_mean.T, new_error


def solution(mesh):
    fine = Mesh(mesh.devices.reshape(NX, NZ, NC, NY), ("x", "z", "c", "y"))
    replicas = ("x", "z", "c")
    in_specs = (P(replicas, None, "y"), P(replicas, None, "y"), P("y", None))
    out_specs = (P(), P("y", None), P(replicas, None, "y"))
    return jax.shard_map(
        on_device, mesh=fine, in_specs=in_specs, out_specs=out_specs, check_vma=False
    )
```

```python
import jax
import jax.numpy as jnp
from jax import lax
from jax.experimental import pallas as pl
from jax.experimental.pallas import tpu as pltpu
from jax.sharding import Mesh, PartitionSpec as P

EPS = 1e-06
NX, NZ, NC, NY = 4, 8, 2, 4
ROWS, R, COLS = 256, 32, 7168
GROUP = R // NZ
BLOCK = COLS // NX
SLOTS = NZ // NC
WIDTH = BLOCK // NC
PARTS = (NZ, GROUP, WIDTH)
REPLICAS = NX * NZ * NC

VMEM = pl.BlockSpec(memory_space=pltpu.VMEM)
HBM = pl.BlockSpec(memory_space=pltpu.HBM)
CHUNK = 512
CHUNKS = COLS // CHUNK
Z_SHIFTS = ((4, 3, 1, 0), (-3, 2, -2, -1))


def params(mib):
    return pltpu.CompilerParams(vmem_limit_bytes=mib * 1024 * 1024)


def merge_kernel(grads_ref, error_ref, q_ref, merged_ref, term_ref, g_buf, e_buf, q_buf, g_sem, e_sem, q_sem):
    def copies(i):
        columns = pl.ds(i * CHUNK, CHUNK)
        return (
            pltpu.make_async_copy(grads_ref.at[0, :, columns], g_buf.at[i], g_sem.at[i]),
            pltpu.make_async_copy(error_ref.at[0, :, columns], e_buf.at[i], e_sem.at[i]),
            pltpu.make_async_copy(q_ref.at[:, columns], q_buf.at[i], q_sem.at[i]),
        )

    for i in range(CHUNKS):
        for copy in copies(i):
            copy.start()
    total = jnp.zeros((R, ROWS), jnp.float32)
    for i in range(CHUNKS):
        for copy in copies(i):
            copy.wait()
        merged = (g_buf[i].astype(jnp.float32) + e_buf[i].astype(jnp.float32)).astype(jnp.bfloat16)
        merged_ref[:, i * CHUNK:(i + 1) * CHUNK] = merged
        total += lax.dot_general(q_buf[i].astype(jnp.bfloat16), merged, (((1,), (1,)), ((), ())),
                                 preferred_element_type=jnp.float32)
    term_ref[...] = total


def merge(grads, error, q_t):
    return pl.pallas_call(
        merge_kernel,
        in_specs=[HBM, HBM, HBM],
        out_specs=[VMEM, VMEM],
        out_shape=[
            pltpu.VMEM((ROWS, COLS), jnp.bfloat16),
            pltpu.VMEM((R, ROWS), jnp.float32),
        ],
        scratch_shapes=[
            pltpu.VMEM((CHUNKS, ROWS, CHUNK), jnp.bfloat16),
            pltpu.VMEM((CHUNKS, ROWS, CHUNK), jnp.bfloat16),
            pltpu.VMEM((CHUNKS, R, CHUNK), jnp.float32),
            pltpu.SemaphoreType.DMA((CHUNKS,)),
            pltpu.SemaphoreType.DMA((CHUNKS,)),
            pltpu.SemaphoreType.DMA((CHUNKS,)),
        ],
        compiler_params=params(24),
        name="merge",
    )(*(pltpu.with_memory_space_constraint(a, pltpu.HBM) for a in (grads, error, q_t)))


def tree(terms):
    while len(terms) > 1:
        terms = [a + b for a, b in zip(terms[::2], terms[1::2])]
    return terms[0]


def z_at(core, slot, sign):
    low, high = Z_SHIFTS[0][slot], Z_SHIFTS[1][slot]
    return (lax.axis_index("z") + jnp.where(core == 0, sign * low, sign * high) + NZ) % NZ


def orthonormal_kernel(own_ref, *refs):
    mine, theirs = refs[:SLOTS], refs[SLOTS:2 * SLOTS]
    basis_ref, half_ref, ring = refs[2 * SLOTS:]
    core = lax.axis_index("c")
    for group, owner in ((mine, core), (theirs, 1 - core)):
        for slot, ref in enumerate(group):
            ring[z_at(owner, slot, -1)] = ref[...]
    ring[lax.axis_index("z")] = own_ref[...]
    total = (ring[0] + ring[1]) + (ring[2] + ring[3])
    total = total + ((ring[4] + ring[5]) + (ring[6] + ring[7]))

    tiles = [total[8 * i:8 * i + 8] for i in range(R // 8)]
    left = list(tiles)
    basis = [jnp.zeros_like(tile) for tile in tiles]
    rows = lax.broadcasted_iota(jnp.int32, (8, 1), 0)
    for column in range(R):
        tile, row = divmod(column, 8)
        vector = left[tile][row:row + 1]
        if column > 0:
            built = (column - 1) // 8 + 1
            taken = None
            for part in basis[:built]:
                term = jnp.sum(part * vector, axis=1, keepdims=True) * part
                taken = term if taken is None else taken + term
            vector = vector - jnp.sum(taken, axis=0, keepdims=True)
        products = [jnp.sum(tiles[later] * vector, axis=1, keepdims=True) for later in range((column + 1) // 8, R // 8)]
        scale = lax.rsqrt(jnp.sum(vector * vector, axis=1, keepdims=True) + EPS)
        basis[tile] = jnp.where(rows == row, vector * scale, basis[tile])
        square = scale * scale
        for later, product in zip(range((column + 1) // 8, R // 8), products):
            left[later] = left[later] - (product * square) * vector
    result = jnp.concatenate(basis, axis=0)
    basis_ref[...] = result
    half_ref[...] = result.astype(jnp.bfloat16)


def small(kernel, out, count, name, *args, scratch=()):
    return pl.pallas_call(
        kernel,
        in_specs=[VMEM] * len(args),
        out_specs=[VMEM] * count,
        out_shape=[pltpu.VMEM(out, jnp.float32)] * count,
        scratch_shapes=list(scratch),
        compiler_params=params(16),
        name=name,
    )(*args)


def orthonormal(own, mine, theirs):
    return pl.pallas_call(
        orthonormal_kernel,
        in_specs=[VMEM] * (1 + 2 * SLOTS),
        out_specs=[VMEM, VMEM],
        out_shape=[
            pltpu.VMEM((R, ROWS), jnp.float32),
            pltpu.VMEM((R, ROWS), jnp.bfloat16),
        ],
        scratch_shapes=[pltpu.VMEM((NZ, R, ROWS), jnp.float32)],
        compiler_params=params(16),
        name="orthonormal",
    )(own, *mine, *theirs)


def right(p_half, merged, blocks_ahead):
    count = len(blocks_ahead)

    def kernel(half_ref, merged_ref, keep_ref, send_ref):
        first, x = lax.axis_index("c") == 0, lax.axis_index("x")
        for i, ahead in enumerate(blocks_ahead):
            columns = pl.ds(pl.multiple_of((x + ahead) % NX * BLOCK, 128), BLOCK)
            term = jnp.dot(half_ref[...], merged_ref[:, columns], preferred_element_type=jnp.float32)
            low, high = term[:, :WIDTH], term[:, WIDTH:]
            keep, send = jnp.where(first, low, high), jnp.where(first, high, low)
            for group in range(NZ):
                keep_ref[i, group] = keep[group * GROUP:(group + 1) * GROUP]
                send_ref[i, group] = send[group * GROUP:(group + 1) * GROUP]

    return small(kernel, (count,) + PARTS, 2, "right", p_half, merged)


def chip_sum_kernel(keep_ref, got_ref, *outs):
    for i, out in enumerate(outs):
        out[...] = keep_ref[i] + got_ref[i]


def x_sum_kernel(two_ref, one_ref, three_ref, own_ref, out_ref):
    out_ref[...] = (own_ref[...] + two_ref[...]) + (one_ref[...] + three_ref[...])


def mean_kernel(terms_ref, out_ref):
    total = tree([terms_ref[i] for i in range(NZ)]) * (1.0 / REPLICAS)
    for i in range(NZ):
        out_ref[i] = total


def split3(value):
    first = value.astype(jnp.bfloat16)
    rest = value - first.astype(jnp.float32)
    second = rest.astype(jnp.bfloat16)
    third = (rest - second.astype(jnp.float32)).astype(jnp.bfloat16)
    return first, second, third


def left_kernel(basis_ref, left_ref, out_ref, sem):
    copy = pltpu.make_async_copy(basis_ref, out_ref, sem)
    copy.start()
    p1, p2, p3 = split3(basis_ref[...])
    left_ref[...] = jnp.concatenate([p1, p1, p2, p2, p1, p3], axis=0).T
    copy.wait()


def left_factor(basis):
    return pl.pallas_call(
        left_kernel,
        in_specs=[VMEM],
        out_specs=[VMEM, HBM],
        out_shape=[pltpu.VMEM((ROWS, 6 * R), jnp.bfloat16), pltpu.HBM((R, ROWS), jnp.float32)],
        scratch_shapes=[pltpu.SemaphoreType.DMA],
        compiler_params=params(16),
        name="left_factor",
    )(basis)


def rewrite(places, values, left, merged, so_far):
    count = len(values)

    def kernel(*refs):
        held, (left_ref, merged_ref) = refs[:count], refs[count:count + 2]
        mean_ref, error_ref, mean_buf, error_buf, mean_sem, error_sem = refs[-6:]
        core, x = lax.axis_index("c"), lax.axis_index("x")
        copies = []
        for i, (behind, away) in enumerate(places):
            owner = 1 - core if away else core
            start = (x - behind + NX) % NX * BLOCK + owner * WIDTH
            columns = pl.ds(pl.multiple_of(start, 128), WIDTH)
            q_mean = jnp.concatenate([held[i][group] for group in range(NZ)], axis=0)
            mean_buf[i] = q_mean
            copies.append(pltpu.make_async_copy(mean_buf.at[i], mean_ref.at[:, columns], mean_sem.at[i]))
            copies[-1].start()
            q1, q2, q3 = split3(q_mean)
            q_all = jnp.concatenate([q1, q2, q1, q2, q3, q1], axis=0)
            approx = jnp.dot(left_ref[...], q_all, preferred_element_type=jnp.float32)
            error_buf[i] = (merged_ref[:, columns].astype(jnp.float32) - approx).astype(jnp.bfloat16)
            copies.append(pltpu.make_async_copy(error_buf.at[i], error_ref.at[0, :, columns], error_sem.at[i]))
            copies[-1].start()
        for copy in copies:
            copy.wait()

    return pl.pallas_call(
        kernel,
        in_specs=[VMEM] * (count + 2) + [HBM] * len(so_far),
        out_specs=[HBM, HBM],
        out_shape=[
            pltpu.HBM((R, COLS), jnp.float32),
            pltpu.HBM((1, ROWS, COLS), jnp.bfloat16),
        ],
        scratch_shapes=[
            pltpu.VMEM((count, R, WIDTH), jnp.float32),
            pltpu.VMEM((count, ROWS, WIDTH), jnp.bfloat16),
            pltpu.SemaphoreType.DMA((count,)),
            pltpu.SemaphoreType.DMA((count,)),
        ],
        input_output_aliases={count + 2 + i: i for i in range(len(so_far))},
        cost_estimate=pl.CostEstimate(flops=2 * count * ROWS * 6 * R * WIDTH, transcendentals=0,
                                      bytes_accessed=4 * count * (ROWS + R) * WIDTH),
        compiler_params=params(16),
        name="rewrite",
    )(*values, left, merged, *so_far)


def shift(value, axis, size, by):
    return lax.ppermute(value, axis, [(i, (i + by) % size) for i in range(size)])


def swap(value, axis, size):
    return lax.ppermute(value, axis, [(i, i ^ 1) for i in range(size)])


def ring4(value, axis, size, unit):
    across = shift(value, axis, size, 2 * unit)
    left = shift(value, axis, size, unit)
    right = shift(value, axis, size, size - unit)
    return (value + across) + (left + right)


def z_round(value, slot):
    pairs = []
    for z in range(NZ):
        for core in range(NC):
            by = Z_SHIFTS[core][slot]
            if by != 0:
                pairs.append((z * NC + core, (z + by) % NZ * NC + core))
    return lax.ppermute(value, ("z", "c"), pairs)


def exchange(value, axes):
    return lax.all_to_all(value, axes, 0, 0, tiled=True)


def x_ring(two, one, three):
    return shift(two, "x", NX, 2), shift(one, "x", NX, 1), shift(three, "x", NX, 3)


def on_device(grads, error, q_in):
    merged, term = merge(grads, error, q_in.T)
    own = term + swap(term, "c", NC)
    own = ring4(own, "y", NY, 1)
    own = ring4(own, "x", NX, 1)
    mine = [z_round(own, slot) for slot in range(SLOTS)]
    theirs = [swap(value, "c", NC) for value in mine]
    basis, p_half = orthonormal(own, mine, theirs)

    keep, send = right(p_half, merged, (2,))
    [two] = small(chip_sum_kernel, PARTS, 1, "chip_sum", keep, swap(send, "c", NC))
    two, p_half = lax.optimization_barrier((two, p_half))
    keep, send = right(p_half, merged, (1, 3, 0))
    one, three, own = small(chip_sum_kernel, PARTS, 3, "chip_sum", keep, swap(send, "c", NC))
    [own] = small(x_sum_kernel, PARTS, 1, "x_sum", *x_ring(two, one, three), own)
    [mean] = small(mean_kernel, PARTS, 1, "mean", exchange(own, "z"))
    own = exchange(mean, "z")

    two, one, three = x_ring(own, own, own)
    left, p_basis = left_factor(basis)
    done = rewrite([(0, 0), (0, 1)], [own, swap(own, "c", NC)], left, merged, [])
    two, *done = lax.optimization_barrier((two, *done))
    far_two = swap(two, "c", NC)
    done = rewrite([(2, 0)], [two], left, merged, done)
    three, one, *done = lax.optimization_barrier((three, one, *done))
    far_three, far_one = swap(three, "c", NC), swap(one, "c", NC)
    done = rewrite([(3, 0), (1, 0), (2, 1)], [three, one, far_two], left, merged, done)
    q_mean, new_error = rewrite([(3, 1), (1, 1)], [far_three, far_one], left, merged, done)
    return p_basis.T, q_mean.T, new_error


def solution(mesh):
    fine = Mesh(mesh.devices.reshape(NX, NZ, NC, NY), ("x", "z", "c", "y"))
    replicas = ("x", "z", "c")
    in_specs = (P(replicas, None, "y"), P(replicas, None, "y"), P("y", None))
    out_specs = (P(), P("y", None), P(replicas, None, "y"))
    return jax.shard_map(
        on_device, mesh=fine, in_specs=in_specs, out_specs=out_specs, check_vma=False
    )
```

```python
import jax
import jax.numpy as jnp
from jax import lax
from jax.experimental import pallas as pl
from jax.experimental.pallas import tpu as pltpu
from jax.sharding import Mesh, PartitionSpec as P

EPS = 1e-06
NX, NZ, NC, NY = 4, 8, 2, 4
ROWS, R, COLS = 256, 32, 7168
GROUP = R // NZ
BLOCK = COLS // NX
SLOTS = NZ // NC
WIDTH = BLOCK // NC
PARTS = (NZ, GROUP, WIDTH)
REPLICAS = NX * NZ * NC

VMEM = pl.BlockSpec(memory_space=pltpu.VMEM)
HBM = pl.BlockSpec(memory_space=pltpu.HBM)
CHUNK = 512
CHUNKS = COLS // CHUNK
Z_SHIFTS = ((4, 3, 1, 0), (-3, 2, -2, -1))


def params(mib):
    return pltpu.CompilerParams(vmem_limit_bytes=mib * 1024 * 1024)


def merge_kernel(grads_ref, error_ref, q_ref, merged_ref, term_ref, g_buf, e_buf, q_buf, g_sem, e_sem, q_sem):
    def copies(i):
        columns = pl.ds(i * CHUNK, CHUNK)
        return (
            pltpu.make_async_copy(grads_ref.at[0, :, columns], g_buf.at[i], g_sem.at[i]),
            pltpu.make_async_copy(error_ref.at[0, :, columns], e_buf.at[i], e_sem.at[i]),
            pltpu.make_async_copy(q_ref.at[:, columns], q_buf.at[i], q_sem.at[i]),
        )

    for i in range(CHUNKS):
        for copy in copies(i):
            copy.start()
    total = jnp.zeros((R, ROWS), jnp.float32)
    for i in range(CHUNKS):
        for copy in copies(i):
            copy.wait()
        merged = (g_buf[i].astype(jnp.float32) + e_buf[i].astype(jnp.float32)).astype(jnp.bfloat16)
        merged_ref[:, i * CHUNK:(i + 1) * CHUNK] = merged
        total += lax.dot_general(q_buf[i].astype(jnp.bfloat16), merged, (((1,), (1,)), ((), ())),
                                 preferred_element_type=jnp.float32)
    term_ref[...] = total


def merge(grads, error, q_t):
    return pl.pallas_call(
        merge_kernel,
        in_specs=[HBM, HBM, HBM],
        out_specs=[VMEM, VMEM],
        out_shape=[
            pltpu.VMEM((ROWS, COLS), jnp.bfloat16),
            pltpu.VMEM((R, ROWS), jnp.float32),
        ],
        scratch_shapes=[
            pltpu.VMEM((CHUNKS, ROWS, CHUNK), jnp.bfloat16),
            pltpu.VMEM((CHUNKS, ROWS, CHUNK), jnp.bfloat16),
            pltpu.VMEM((CHUNKS, R, CHUNK), jnp.float32),
            pltpu.SemaphoreType.DMA((CHUNKS,)),
            pltpu.SemaphoreType.DMA((CHUNKS,)),
            pltpu.SemaphoreType.DMA((CHUNKS,)),
        ],
        compiler_params=params(24),
        name="merge",
    )(*(pltpu.with_memory_space_constraint(a, pltpu.HBM) for a in (grads, error, q_t)))


def tree(terms):
    while len(terms) > 1:
        terms = [a + b for a, b in zip(terms[::2], terms[1::2])]
    return terms[0]


def z_at(core, slot, sign):
    low, high = Z_SHIFTS[0][slot], Z_SHIFTS[1][slot]
    return (lax.axis_index("z") + jnp.where(core == 0, sign * low, sign * high) + NZ) % NZ


def orthonormal_kernel(own_ref, *refs):
    mine, theirs = refs[:SLOTS], refs[SLOTS:2 * SLOTS]
    basis_ref, half_ref, ring = refs[2 * SLOTS:]
    core = lax.axis_index("c")
    for group, owner in ((mine, core), (theirs, 1 - core)):
        for slot, ref in enumerate(group):
            ring[z_at(owner, slot, -1)] = ref[...]
    ring[lax.axis_index("z")] = own_ref[...]
    total = (ring[0] + ring[1]) + (ring[2] + ring[3])
    total = total + ((ring[4] + ring[5]) + (ring[6] + ring[7]))

    tiles = [total[8 * i:8 * i + 8] for i in range(R // 8)]
    left = list(tiles)
    basis = [jnp.zeros_like(tile) for tile in tiles]
    rows = lax.broadcasted_iota(jnp.int32, (8, 1), 0)
    for column in range(R):
        tile, row = divmod(column, 8)
        vector = left[tile][row:row + 1]
        if column > 0:
            built = (column - 1) // 8 + 1
            taken = None
            for part in basis[:built]:
                term = jnp.sum(part * vector, axis=1, keepdims=True) * part
                taken = term if taken is None else taken + term
            vector = vector - jnp.sum(taken, axis=0, keepdims=True)
        products = [jnp.sum(tiles[later] * vector, axis=1, keepdims=True) for later in range((column + 1) // 8, R // 8)]
        scale = lax.rsqrt(jnp.sum(vector * vector, axis=1, keepdims=True) + EPS)
        basis[tile] = jnp.where(rows == row, vector * scale, basis[tile])
        square = scale * scale
        for later, product in zip(range((column + 1) // 8, R // 8), products):
            left[later] = left[later] - (product * square) * vector
    result = jnp.concatenate(basis, axis=0)
    basis_ref[...] = result
    half_ref[...] = result.astype(jnp.bfloat16)


def small(kernel, out, count, name, *args, scratch=()):
    return pl.pallas_call(
        kernel,
        in_specs=[VMEM] * len(args),
        out_specs=[VMEM] * count,
        out_shape=[pltpu.VMEM(out, jnp.float32)] * count,
        scratch_shapes=list(scratch),
        compiler_params=params(16),
        name=name,
    )(*args)


def orthonormal(own, mine, theirs):
    return pl.pallas_call(
        orthonormal_kernel,
        in_specs=[VMEM] * (1 + 2 * SLOTS),
        out_specs=[VMEM, VMEM],
        out_shape=[
            pltpu.VMEM((R, ROWS), jnp.float32),
            pltpu.VMEM((R, ROWS), jnp.bfloat16),
        ],
        scratch_shapes=[pltpu.VMEM((NZ, R, ROWS), jnp.float32)],
        compiler_params=params(16),
        name="orthonormal",
    )(own, *mine, *theirs)


def right(p_half, merged, blocks_ahead):
    count = len(blocks_ahead)

    def kernel(half_ref, merged_ref, keep_ref, send_ref):
        first, x = lax.axis_index("c") == 0, lax.axis_index("x")
        for i, ahead in enumerate(blocks_ahead):
            columns = pl.ds(pl.multiple_of((x + ahead) % NX * BLOCK, 128), BLOCK)
            term = jnp.dot(half_ref[...], merged_ref[:, columns], preferred_element_type=jnp.float32)
            low, high = term[:, :WIDTH], term[:, WIDTH:]
            keep, send = jnp.where(first, low, high), jnp.where(first, high, low)
            for group in range(NZ):
                keep_ref[i, group] = keep[group * GROUP:(group + 1) * GROUP]
                send_ref[i, group] = send[group * GROUP:(group + 1) * GROUP]

    return small(kernel, (count,) + PARTS, 2, "right", p_half, merged)


def chip_sum_kernel(keep_ref, got_ref, *outs):
    for i, out in enumerate(outs):
        out[...] = keep_ref[i] + got_ref[i]


def x_sum_kernel(two_ref, one_ref, three_ref, own_ref, out_ref):
    out_ref[...] = (own_ref[...] + two_ref[...]) + (one_ref[...] + three_ref[...])


def mean_kernel(terms_ref, out_ref):
    total = tree([terms_ref[i] for i in range(NZ)]) * (1.0 / REPLICAS)
    for i in range(NZ):
        out_ref[i] = total


def split3(value):
    first = value.astype(jnp.bfloat16)
    rest = value - first.astype(jnp.float32)
    second = rest.astype(jnp.bfloat16)
    third = (rest - second.astype(jnp.float32)).astype(jnp.bfloat16)
    return first, second, third


def left_kernel(basis_ref, left_ref, out_ref, sem):
    copy = pltpu.make_async_copy(basis_ref, out_ref, sem)
    copy.start()
    p1, p2, p3 = split3(basis_ref[...])
    left_ref[...] = jnp.concatenate([p1, p1, p2, p2, p1, p3], axis=0).T
    copy.wait()


def left_factor(basis):
    return pl.pallas_call(
        left_kernel,
        in_specs=[VMEM],
        out_specs=[VMEM, HBM],
        out_shape=[pltpu.VMEM((ROWS, 6 * R), jnp.bfloat16), pltpu.HBM((R, ROWS), jnp.float32)],
        scratch_shapes=[pltpu.SemaphoreType.DMA],
        compiler_params=params(16),
        name="left_factor",
    )(basis)


def rewrite(places, values, left, merged, so_far):
    count = len(values)

    def kernel(*refs):
        held, (left_ref, merged_ref) = refs[:count], refs[count:count + 2]
        mean_ref, error_ref, mean_buf, error_buf, mean_sem, error_sem = refs[-6:]
        core, x = lax.axis_index("c"), lax.axis_index("x")
        copies = []
        for i, (behind, away) in enumerate(places):
            owner = 1 - core if away else core
            start = (x - behind + NX) % NX * BLOCK + owner * WIDTH
            columns = pl.ds(pl.multiple_of(start, 128), WIDTH)
            q_mean = jnp.concatenate([held[i][group] for group in range(NZ)], axis=0)
            mean_buf[i] = q_mean
            copies.append(pltpu.make_async_copy(mean_buf.at[i], mean_ref.at[:, columns], mean_sem.at[i]))
            copies[-1].start()
            q1, q2, q3 = split3(q_mean)
            q_all = jnp.concatenate([q1, q2, q1, q2, q3, q1], axis=0)
            approx = jnp.dot(left_ref[...], q_all, preferred_element_type=jnp.float32)
            error_buf[i] = (merged_ref[:, columns].astype(jnp.float32) - approx).astype(jnp.bfloat16)
            copies.append(pltpu.make_async_copy(error_buf.at[i], error_ref.at[0, :, columns], error_sem.at[i]))
            copies[-1].start()
        for copy in copies:
            copy.wait()

    return pl.pallas_call(
        kernel,
        in_specs=[VMEM] * (count + 2) + [HBM] * len(so_far),
        out_specs=[HBM, HBM],
        out_shape=[
            pltpu.HBM((R, COLS), jnp.float32),
            pltpu.HBM((1, ROWS, COLS), jnp.bfloat16),
        ],
        scratch_shapes=[
            pltpu.VMEM((count, R, WIDTH), jnp.float32),
            pltpu.VMEM((count, ROWS, WIDTH), jnp.bfloat16),
            pltpu.SemaphoreType.DMA((count,)),
            pltpu.SemaphoreType.DMA((count,)),
        ],
        input_output_aliases={count + 2 + i: i for i in range(len(so_far))},
        cost_estimate=pl.CostEstimate(flops=2 * count * ROWS * 6 * R * WIDTH, transcendentals=0,
                                      bytes_accessed=4 * count * (ROWS + R) * WIDTH),
        compiler_params=params(16),
        name="rewrite",
    )(*values, left, merged, *so_far)


def shift(value, axis, size, by):
    return lax.ppermute(value, axis, [(i, (i + by) % size) for i in range(size)])


def swap(value, axis, size):
    return lax.ppermute(value, axis, [(i, i ^ 1) for i in range(size)])


def ring4(value, axis, size, unit):
    across = shift(value, axis, size, 2 * unit)
    left = shift(value, axis, size, unit)
    right = shift(value, axis, size, size - unit)
    return (value + across) + (left + right)


def z_round(value, slot):
    pairs = []
    for z in range(NZ):
        for core in range(NC):
            by = Z_SHIFTS[core][slot]
            if by != 0:
                pairs.append((z * NC + core, (z + by) % NZ * NC + core))
    return lax.ppermute(value, ("z", "c"), pairs)


def exchange(value, axes):
    return lax.all_to_all(value, axes, 0, 0, tiled=True)


def x_ring(two, one, three):
    return shift(two, "x", NX, 2), shift(one, "x", NX, 1), shift(three, "x", NX, 3)


def on_device(grads, error, q_in):
    merged, term = merge(grads, error, q_in.T)
    own = term + swap(term, "c", NC)
    own = ring4(own, "y", NY, 1)
    own = ring4(own, "x", NX, 1)
    mine = [z_round(own, slot) for slot in range(SLOTS)]
    theirs = [swap(value, "c", NC) for value in mine]
    basis, p_half = orthonormal(own, mine, theirs)

    keep, send = right(p_half, merged, (2,))
    [two] = small(chip_sum_kernel, PARTS, 1, "chip_sum", keep, swap(send, "c", NC))
    two, p_half = lax.optimization_barrier((two, p_half))
    keep, send = right(p_half, merged, (1, 3, 0))
    one, three, own = small(chip_sum_kernel, PARTS, 3, "chip_sum", keep, swap(send, "c", NC))
    [own] = small(x_sum_kernel, PARTS, 1, "x_sum", *x_ring(two, one, three), own)
    [mean] = small(mean_kernel, PARTS, 1, "mean", exchange(own, "z"))
    own = exchange(mean, "z")

    two, one, three = x_ring(own, own, own)
    left, p_basis = left_factor(basis)
    done = rewrite([(0, 0)], [own], left, merged, [])
    two, own, *done = lax.optimization_barrier((two, own, *done))
    far_two, far_own = swap(two, "c", NC), swap(own, "c", NC)
    done = rewrite([(2, 0)], [two], left, merged, done)
    three, one, *done = lax.optimization_barrier((three, one, *done))
    far_three, far_one = swap(three, "c", NC), swap(one, "c", NC)
    done = rewrite([(3, 0), (1, 0), (2, 1), (0, 1)], [three, one, far_two, far_own], left, merged, done)
    q_mean, new_error = rewrite([(3, 1), (1, 1)], [far_three, far_one], left, merged, done)
    return p_basis.T, q_mean.T, new_error


def solution(mesh):
    fine = Mesh(mesh.devices.reshape(NX, NZ, NC, NY), ("x", "z", "c", "y"))
    replicas = ("x", "z", "c")
    in_specs = (P(replicas, None, "y"), P(replicas, None, "y"), P("y", None))
    out_specs = (P(), P("y", None), P(replicas, None, "y"))
    return jax.shard_map(
        on_device, mesh=fine, in_specs=in_specs, out_specs=out_specs, check_vma=False
    )
```

```python
import jax
import jax.numpy as jnp
from jax import lax
from jax.experimental import pallas as pl
from jax.experimental.pallas import tpu as pltpu
from jax.sharding import Mesh, PartitionSpec as P

EPS = 1e-06
NX, NZ, NC, NY = 4, 8, 2, 4
ROWS, R, COLS = 256, 32, 7168
GROUP = R // NZ
BLOCK = COLS // NX
SLOTS = NZ // NC
WIDTH = BLOCK // NC
PARTS = (NZ, GROUP, WIDTH)
REPLICAS = NX * NZ * NC

VMEM = pl.BlockSpec(memory_space=pltpu.VMEM)
HBM = pl.BlockSpec(memory_space=pltpu.HBM)
CHUNK = 1024
CHUNKS = COLS // CHUNK
Z_SHIFTS = ((4, 3, 1, 0), (-3, 2, -2, -1))


def params(mib):
    return pltpu.CompilerParams(vmem_limit_bytes=mib * 1024 * 1024)


def merge_kernel(grads_ref, error_ref, q_ref, merged_ref, term_ref, g_buf, e_buf, q_buf, g_sem, e_sem, q_sem):
    def copies(i):
        columns = pl.ds(i * CHUNK, CHUNK)
        return (
            pltpu.make_async_copy(grads_ref.at[0, :, columns], g_buf.at[i], g_sem.at[i]),
            pltpu.make_async_copy(error_ref.at[0, :, columns], e_buf.at[i], e_sem.at[i]),
            pltpu.make_async_copy(q_ref.at[:, columns], q_buf.at[i], q_sem.at[i]),
        )

    for i in range(CHUNKS):
        for copy in copies(i):
            copy.start()
    total = jnp.zeros((R, ROWS), jnp.float32)
    for i in range(CHUNKS):
        for copy in copies(i):
            copy.wait()
        merged = (g_buf[i].astype(jnp.float32) + e_buf[i].astype(jnp.float32)).astype(jnp.bfloat16)
        merged_ref[:, i * CHUNK:(i + 1) * CHUNK] = merged
        total += lax.dot_general(q_buf[i].astype(jnp.bfloat16), merged, (((1,), (1,)), ((), ())),
                                 preferred_element_type=jnp.float32)
    term_ref[...] = total


def merge(grads, error, q_t):
    return pl.pallas_call(
        merge_kernel,
        in_specs=[HBM, HBM, HBM],
        out_specs=[VMEM, VMEM],
        out_shape=[
            pltpu.VMEM((ROWS, COLS), jnp.bfloat16),
            pltpu.VMEM((R, ROWS), jnp.float32),
        ],
        scratch_shapes=[
            pltpu.VMEM((CHUNKS, ROWS, CHUNK), jnp.bfloat16),
            pltpu.VMEM((CHUNKS, ROWS, CHUNK), jnp.bfloat16),
            pltpu.VMEM((CHUNKS, R, CHUNK), jnp.float32),
            pltpu.SemaphoreType.DMA((CHUNKS,)),
            pltpu.SemaphoreType.DMA((CHUNKS,)),
            pltpu.SemaphoreType.DMA((CHUNKS,)),
        ],
        compiler_params=params(24),
        name="merge",
    )(*(pltpu.with_memory_space_constraint(a, pltpu.HBM) for a in (grads, error, q_t)))


def tree(terms):
    while len(terms) > 1:
        terms = [a + b for a, b in zip(terms[::2], terms[1::2])]
    return terms[0]


def z_at(core, slot, sign):
    low, high = Z_SHIFTS[0][slot], Z_SHIFTS[1][slot]
    return (lax.axis_index("z") + jnp.where(core == 0, sign * low, sign * high) + NZ) % NZ


def orthonormal_kernel(own_ref, *refs):
    mine, theirs = refs[:SLOTS], refs[SLOTS:2 * SLOTS]
    basis_ref, half_ref, ring = refs[2 * SLOTS:]
    core = lax.axis_index("c")
    for group, owner in ((mine, core), (theirs, 1 - core)):
        for slot, ref in enumerate(group):
            ring[z_at(owner, slot, -1)] = ref[...]
    ring[lax.axis_index("z")] = own_ref[...]
    total = (ring[0] + ring[1]) + (ring[2] + ring[3])
    total = total + ((ring[4] + ring[5]) + (ring[6] + ring[7]))

    tiles = [total[8 * i:8 * i + 8] for i in range(R // 8)]
    left = list(tiles)
    basis = [jnp.zeros_like(tile) for tile in tiles]
    rows = lax.broadcasted_iota(jnp.int32, (8, 1), 0)
    for column in range(R):
        tile, row = divmod(column, 8)
        vector = left[tile][row:row + 1]
        if column > 0:
            built = (column - 1) // 8 + 1
            taken = None
            for part in basis[:built]:
                term = jnp.sum(part * vector, axis=1, keepdims=True) * part
                taken = term if taken is None else taken + term
            vector = vector - jnp.sum(taken, axis=0, keepdims=True)
        products = [jnp.sum(tiles[later] * vector, axis=1, keepdims=True) for later in range((column + 1) // 8, R // 8)]
        scale = lax.rsqrt(jnp.sum(vector * vector, axis=1, keepdims=True) + EPS)
        basis[tile] = jnp.where(rows == row, vector * scale, basis[tile])
        square = scale * scale
        for later, product in zip(range((column + 1) // 8, R // 8), products):
            left[later] = left[later] - (product * square) * vector
    result = jnp.concatenate(basis, axis=0)
    basis_ref[...] = result
    half_ref[...] = result.astype(jnp.bfloat16)


def small(kernel, out, count, name, *args, scratch=()):
    return pl.pallas_call(
        kernel,
        in_specs=[VMEM] * len(args),
        out_specs=[VMEM] * count,
        out_shape=[pltpu.VMEM(out, jnp.float32)] * count,
        scratch_shapes=list(scratch),
        compiler_params=params(16),
        name=name,
    )(*args)


def orthonormal(own, mine, theirs):
    return pl.pallas_call(
        orthonormal_kernel,
        in_specs=[VMEM] * (1 + 2 * SLOTS),
        out_specs=[VMEM, VMEM],
        out_shape=[
            pltpu.VMEM((R, ROWS), jnp.float32),
            pltpu.VMEM((R, ROWS), jnp.bfloat16),
        ],
        scratch_shapes=[pltpu.VMEM((NZ, R, ROWS), jnp.float32)],
        compiler_params=params(16),
        name="orthonormal",
    )(own, *mine, *theirs)


def right(p_half, merged, blocks_ahead):
    count = len(blocks_ahead)

    def kernel(half_ref, merged_ref, keep_ref, send_ref):
        first, x = lax.axis_index("c") == 0, lax.axis_index("x")
        for i, ahead in enumerate(blocks_ahead):
            columns = pl.ds(pl.multiple_of((x + ahead) % NX * BLOCK, 128), BLOCK)
            term = jnp.dot(half_ref[...], merged_ref[:, columns], preferred_element_type=jnp.float32)
            low, high = term[:, :WIDTH], term[:, WIDTH:]
            keep, send = jnp.where(first, low, high), jnp.where(first, high, low)
            for group in range(NZ):
                keep_ref[i, group] = keep[group * GROUP:(group + 1) * GROUP]
                send_ref[i, group] = send[group * GROUP:(group + 1) * GROUP]

    return small(kernel, (count,) + PARTS, 2, "right", p_half, merged)


def chip_sum_kernel(keep_ref, got_ref, *outs):
    for i, out in enumerate(outs):
        out[...] = keep_ref[i] + got_ref[i]


def x_sum_kernel(two_ref, one_ref, three_ref, own_ref, out_ref):
    out_ref[...] = (own_ref[...] + two_ref[...]) + (one_ref[...] + three_ref[...])


def mean_kernel(terms_ref, out_ref):
    total = tree([terms_ref[i] for i in range(NZ)]) * (1.0 / REPLICAS)
    for i in range(NZ):
        out_ref[i] = total


def split3(value):
    first = value.astype(jnp.bfloat16)
    rest = value - first.astype(jnp.float32)
    second = rest.astype(jnp.bfloat16)
    third = (rest - second.astype(jnp.float32)).astype(jnp.bfloat16)
    return first, second, third


def left_kernel(basis_ref, left_ref, out_ref, sem):
    copy = pltpu.make_async_copy(basis_ref, out_ref, sem)
    copy.start()
    p1, p2, p3 = split3(basis_ref[...])
    left_ref[...] = jnp.concatenate([p1, p1, p2, p2, p1, p3], axis=0).T
    copy.wait()


def left_factor(basis):
    return pl.pallas_call(
        left_kernel,
        in_specs=[VMEM],
        out_specs=[VMEM, HBM],
        out_shape=[pltpu.VMEM((ROWS, 6 * R), jnp.bfloat16), pltpu.HBM((R, ROWS), jnp.float32)],
        scratch_shapes=[pltpu.SemaphoreType.DMA],
        compiler_params=params(16),
        name="left_factor",
    )(basis)


def rewrite(places, values, left, merged, so_far):
    count = len(values)

    def kernel(*refs):
        held, (left_ref, merged_ref) = refs[:count], refs[count:count + 2]
        mean_ref, error_ref, mean_buf, error_buf, mean_sem, error_sem = refs[-6:]
        core, x = lax.axis_index("c"), lax.axis_index("x")
        copies = []
        for i, (behind, away) in enumerate(places):
            owner = 1 - core if away else core
            start = (x - behind + NX) % NX * BLOCK + owner * WIDTH
            columns = pl.ds(pl.multiple_of(start, 128), WIDTH)
            q_mean = jnp.concatenate([held[i][group] for group in range(NZ)], axis=0)
            mean_buf[i] = q_mean
            copies.append(pltpu.make_async_copy(mean_buf.at[i], mean_ref.at[:, columns], mean_sem.at[i]))
            copies[-1].start()
            q1, q2, q3 = split3(q_mean)
            q_all = jnp.concatenate([q1, q2, q1, q2, q3, q1], axis=0)
            approx = jnp.dot(left_ref[...], q_all, preferred_element_type=jnp.float32)
            error_buf[i] = (merged_ref[:, columns].astype(jnp.float32) - approx).astype(jnp.bfloat16)
            copies.append(pltpu.make_async_copy(error_buf.at[i], error_ref.at[0, :, columns], error_sem.at[i]))
            copies[-1].start()
        for copy in copies:
            copy.wait()

    return pl.pallas_call(
        kernel,
        in_specs=[VMEM] * (count + 2) + [HBM] * len(so_far),
        out_specs=[HBM, HBM],
        out_shape=[
            pltpu.HBM((R, COLS), jnp.float32),
            pltpu.HBM((1, ROWS, COLS), jnp.bfloat16),
        ],
        scratch_shapes=[
            pltpu.VMEM((count, R, WIDTH), jnp.float32),
            pltpu.VMEM((count, ROWS, WIDTH), jnp.bfloat16),
            pltpu.SemaphoreType.DMA((count,)),
            pltpu.SemaphoreType.DMA((count,)),
        ],
        input_output_aliases={count + 2 + i: i for i in range(len(so_far))},
        cost_estimate=pl.CostEstimate(flops=2 * count * ROWS * 6 * R * WIDTH, transcendentals=0,
                                      bytes_accessed=4 * count * (ROWS + R) * WIDTH),
        compiler_params=params(16),
        name="rewrite",
    )(*values, left, merged, *so_far)


def shift(value, axis, size, by):
    return lax.ppermute(value, axis, [(i, (i + by) % size) for i in range(size)])


def swap(value, axis, size):
    return lax.ppermute(value, axis, [(i, i ^ 1) for i in range(size)])


def ring4(value, axis, size, unit):
    across = shift(value, axis, size, 2 * unit)
    left = shift(value, axis, size, unit)
    right = shift(value, axis, size, size - unit)
    return (value + across) + (left + right)


def z_round(value, slot):
    pairs = []
    for z in range(NZ):
        for core in range(NC):
            by = Z_SHIFTS[core][slot]
            if by != 0:
                pairs.append((z * NC + core, (z + by) % NZ * NC + core))
    return lax.ppermute(value, ("z", "c"), pairs)


def exchange(value, axes):
    return lax.all_to_all(value, axes, 0, 0, tiled=True)


def x_ring(two, one, three):
    return shift(two, "x", NX, 2), shift(one, "x", NX, 1), shift(three, "x", NX, 3)


def on_device(grads, error, q_in):
    merged, term = merge(grads, error, q_in.T)
    own = term + swap(term, "c", NC)
    own = ring4(own, "y", NY, 1)
    own = ring4(own, "x", NX, 1)
    mine = [z_round(own, slot) for slot in range(SLOTS)]
    theirs = [swap(value, "c", NC) for value in mine]
    basis, p_half = orthonormal(own, mine, theirs)

    keep, send = right(p_half, merged, (2,))
    [two] = small(chip_sum_kernel, PARTS, 1, "chip_sum", keep, swap(send, "c", NC))
    two, p_half = lax.optimization_barrier((two, p_half))
    keep, send = right(p_half, merged, (1, 3, 0))
    one, three, own = small(chip_sum_kernel, PARTS, 3, "chip_sum", keep, swap(send, "c", NC))
    [own] = small(x_sum_kernel, PARTS, 1, "x_sum", *x_ring(two, one, three), own)
    [mean] = small(mean_kernel, PARTS, 1, "mean", exchange(own, "z"))
    own = exchange(mean, "z")

    two, one, three = x_ring(own, own, own)
    left, p_basis = left_factor(basis)
    done = rewrite([(0, 0)], [own], left, merged, [])
    two, own, *done = lax.optimization_barrier((two, own, *done))
    far_two, far_own = swap(two, "c", NC), swap(own, "c", NC)
    done = rewrite([(2, 0)], [two], left, merged, done)
    three, one, *done = lax.optimization_barrier((three, one, *done))
    far_three, far_one = swap(three, "c", NC), swap(one, "c", NC)
    done = rewrite([(3, 0), (1, 0), (2, 1), (0, 1)], [three, one, far_two, far_own], left, merged, done)
    q_mean, new_error = rewrite([(3, 1), (1, 1)], [far_three, far_one], left, merged, done)
    return p_basis.T, q_mean.T, new_error


def solution(mesh):
    fine = Mesh(mesh.devices.reshape(NX, NZ, NC, NY), ("x", "z", "c", "y"))
    replicas = ("x", "z", "c")
    in_specs = (P(replicas, None, "y"), P(replicas, None, "y"), P("y", None))
    out_specs = (P(), P("y", None), P(replicas, None, "y"))
    return jax.shard_map(
        on_device, mesh=fine, in_specs=in_specs, out_specs=out_specs, check_vma=False
    )
```

```python
import jax
import jax.numpy as jnp
from jax import lax
from jax.experimental import pallas as pl
from jax.experimental.pallas import tpu as pltpu
from jax.sharding import Mesh, PartitionSpec as P

EPS = 1e-06
NX, NZ, NC, NY = 4, 8, 2, 4
ROWS, R, COLS = 256, 32, 7168
GROUP = R // NZ
BLOCK = COLS // NX
SLOTS = NZ // NC
WIDTH = BLOCK // NC
PARTS = (NZ, GROUP, WIDTH)
REPLICAS = NX * NZ * NC

VMEM = pl.BlockSpec(memory_space=pltpu.VMEM)
HBM = pl.BlockSpec(memory_space=pltpu.HBM)
CHUNK = 1024
CHUNKS = COLS // CHUNK
Z_SHIFTS = ((4, 3, 1, 0), (-3, 2, -2, -1))


def params(mib):
    return pltpu.CompilerParams(vmem_limit_bytes=mib * 1024 * 1024)


def merge_kernel(grads_ref, error_ref, q_ref, merged_ref, term_ref, g_buf, e_buf, q_buf, g_sem, e_sem, q_sem):
    def copies(i):
        columns = pl.ds(i * CHUNK, CHUNK)
        return (
            pltpu.make_async_copy(grads_ref.at[0, :, columns], g_buf.at[i], g_sem.at[i]),
            pltpu.make_async_copy(error_ref.at[0, :, columns], e_buf.at[i], e_sem.at[i]),
            pltpu.make_async_copy(q_ref.at[:, columns], q_buf.at[i], q_sem.at[i]),
        )

    for i in range(CHUNKS):
        for copy in copies(i):
            copy.start()
    total = jnp.zeros((R, ROWS), jnp.float32)
    for i in range(CHUNKS):
        for copy in copies(i):
            copy.wait()
        merged = (g_buf[i].astype(jnp.float32) + e_buf[i].astype(jnp.float32)).astype(jnp.bfloat16)
        merged_ref[:, i * CHUNK:(i + 1) * CHUNK] = merged
        total += lax.dot_general(q_buf[i].astype(jnp.bfloat16), merged, (((1,), (1,)), ((), ())),
                                 preferred_element_type=jnp.float32)
    term_ref[...] = total


def merge(grads, error, q_t):
    return pl.pallas_call(
        merge_kernel,
        in_specs=[HBM, HBM, HBM],
        out_specs=[VMEM, VMEM],
        out_shape=[
            pltpu.VMEM((ROWS, COLS), jnp.bfloat16),
            pltpu.VMEM((R, ROWS), jnp.float32),
        ],
        scratch_shapes=[
            pltpu.VMEM((CHUNKS, ROWS, CHUNK), jnp.bfloat16),
            pltpu.VMEM((CHUNKS, ROWS, CHUNK), jnp.bfloat16),
            pltpu.VMEM((CHUNKS, R, CHUNK), jnp.float32),
            pltpu.SemaphoreType.DMA((CHUNKS,)),
            pltpu.SemaphoreType.DMA((CHUNKS,)),
            pltpu.SemaphoreType.DMA((CHUNKS,)),
        ],
        compiler_params=params(24),
        name="merge",
    )(*(pltpu.with_memory_space_constraint(a, pltpu.HBM) for a in (grads, error, q_t)))


def tree(terms):
    while len(terms) > 1:
        terms = [a + b for a, b in zip(terms[::2], terms[1::2])]
    return terms[0]


def z_at(core, slot, sign):
    low, high = Z_SHIFTS[0][slot], Z_SHIFTS[1][slot]
    return (lax.axis_index("z") + jnp.where(core == 0, sign * low, sign * high) + NZ) % NZ


def orthonormal_kernel(own_ref, *refs):
    mine, theirs = refs[:SLOTS], refs[SLOTS:2 * SLOTS]
    basis_ref, half_ref, ring = refs[2 * SLOTS:]
    core = lax.axis_index("c")
    for group, owner in ((mine, core), (theirs, 1 - core)):
        for slot, ref in enumerate(group):
            ring[z_at(owner, slot, -1)] = ref[...]
    ring[lax.axis_index("z")] = own_ref[...]
    total = (ring[0] + ring[1]) + (ring[2] + ring[3])
    total = total + ((ring[4] + ring[5]) + (ring[6] + ring[7]))

    tiles = [total[8 * i:8 * i + 8] for i in range(R // 8)]
    left = list(tiles)
    basis = [jnp.zeros_like(tile) for tile in tiles]
    rows = lax.broadcasted_iota(jnp.int32, (8, 1), 0)
    for column in range(R):
        tile, row = divmod(column, 8)
        vector = left[tile][row:row + 1]
        if column > 0:
            built = (column - 1) // 8 + 1
            taken = None
            for part in basis[:built]:
                term = jnp.sum(part * vector, axis=1, keepdims=True) * part
                taken = term if taken is None else taken + term
            vector = vector - jnp.sum(taken, axis=0, keepdims=True)
        products = [jnp.sum(tiles[later] * vector, axis=1, keepdims=True) for later in range((column + 1) // 8, R // 8)]
        scale = lax.rsqrt(jnp.sum(vector * vector, axis=1, keepdims=True) + EPS)
        basis[tile] = jnp.where(rows == row, vector * scale, basis[tile])
        square = scale * scale
        for later, product in zip(range((column + 1) // 8, R // 8), products):
            left[later] = left[later] - (product * square) * vector
    result = jnp.concatenate(basis, axis=0)
    basis_ref[...] = result
    half_ref[...] = result.astype(jnp.bfloat16)


def small(kernel, out, count, name, *args, scratch=()):
    return pl.pallas_call(
        kernel,
        in_specs=[VMEM] * len(args),
        out_specs=[VMEM] * count,
        out_shape=[pltpu.VMEM(out, jnp.float32)] * count,
        scratch_shapes=list(scratch),
        compiler_params=params(16),
        name=name,
    )(*args)


def orthonormal(own, mine, theirs):
    return pl.pallas_call(
        orthonormal_kernel,
        in_specs=[VMEM] * (1 + 2 * SLOTS),
        out_specs=[VMEM, VMEM],
        out_shape=[
            pltpu.VMEM((R, ROWS), jnp.float32),
            pltpu.VMEM((R, ROWS), jnp.bfloat16),
        ],
        scratch_shapes=[pltpu.VMEM((NZ, R, ROWS), jnp.float32)],
        compiler_params=params(16),
        name="orthonormal",
    )(own, *mine, *theirs)


def right(p_half, merged, blocks_ahead):
    count = len(blocks_ahead)

    def kernel(half_ref, merged_ref, keep_ref, send_ref):
        first, x = lax.axis_index("c") == 0, lax.axis_index("x")
        for i, ahead in enumerate(blocks_ahead):
            columns = pl.ds(pl.multiple_of((x + ahead) % NX * BLOCK, 128), BLOCK)
            term = jnp.dot(half_ref[...], merged_ref[:, columns], preferred_element_type=jnp.float32)
            low, high = term[:, :WIDTH], term[:, WIDTH:]
            keep, send = jnp.where(first, low, high), jnp.where(first, high, low)
            for group in range(NZ):
                keep_ref[i, group] = keep[group * GROUP:(group + 1) * GROUP]
                send_ref[i, group] = send[group * GROUP:(group + 1) * GROUP]

    return small(kernel, (count,) + PARTS, 2, "right", p_half, merged)


def chip_sum_kernel(keep_ref, got_ref, *outs):
    for i, out in enumerate(outs):
        out[...] = keep_ref[i] + got_ref[i]


def x_sum_kernel(two_ref, one_ref, three_ref, own_ref, out_ref):
    out_ref[...] = (own_ref[...] + two_ref[...]) + (one_ref[...] + three_ref[...])


def mean_kernel(terms_ref, out_ref):
    total = tree([terms_ref[i] for i in range(NZ)]) * (1.0 / REPLICAS)
    for i in range(NZ):
        out_ref[i] = total


def split3(value):
    first = value.astype(jnp.bfloat16)
    rest = value - first.astype(jnp.float32)
    second = rest.astype(jnp.bfloat16)
    third = (rest - second.astype(jnp.float32)).astype(jnp.bfloat16)
    return first, second, third


def left_kernel(basis_ref, left_ref, out_ref, sem):
    copy = pltpu.make_async_copy(basis_ref, out_ref, sem)
    copy.start()
    p1, p2, p3 = split3(basis_ref[...])
    left_ref[...] = jnp.concatenate([p1, p1, p2, p2, p1, p3], axis=0).T
    copy.wait()


def left_factor(basis):
    return pl.pallas_call(
        left_kernel,
        in_specs=[VMEM],
        out_specs=[VMEM, HBM],
        out_shape=[pltpu.VMEM((ROWS, 6 * R), jnp.bfloat16), pltpu.HBM((R, ROWS), jnp.float32)],
        scratch_shapes=[pltpu.SemaphoreType.DMA],
        compiler_params=params(16),
        name="left_factor",
    )(basis)


def rewrite(places, values, left, merged, so_far):
    count = len(values)

    def kernel(*refs):
        held, (left_ref, merged_ref) = refs[:count], refs[count:count + 2]
        mean_ref, error_ref, mean_buf, error_buf, mean_sem, error_sem = refs[-6:]
        core, x = lax.axis_index("c"), lax.axis_index("x")
        copies = []
        for i, (behind, away) in enumerate(places):
            owner = 1 - core if away else core
            start = (x - behind + NX) % NX * BLOCK + owner * WIDTH
            columns = pl.ds(pl.multiple_of(start, 128), WIDTH)
            q_mean = jnp.concatenate([held[i][group] for group in range(NZ)], axis=0)
            mean_buf[i] = q_mean
            copies.append(pltpu.make_async_copy(mean_buf.at[i], mean_ref.at[:, columns], mean_sem.at[i]))
            copies[-1].start()
            q1, q2, q3 = split3(q_mean)
            q_all = jnp.concatenate([q1, q2, q1, q2, q3, q1], axis=0)
            approx = jnp.dot(left_ref[...], q_all, preferred_element_type=jnp.float32)
            error_buf[i] = (merged_ref[:, columns].astype(jnp.float32) - approx).astype(jnp.bfloat16)
            copies.append(pltpu.make_async_copy(error_buf.at[i], error_ref.at[0, :, columns], error_sem.at[i]))
            copies[-1].start()
        for copy in copies:
            copy.wait()

    return pl.pallas_call(
        kernel,
        in_specs=[VMEM] * (count + 2) + [HBM] * len(so_far),
        out_specs=[HBM, HBM],
        out_shape=[
            pltpu.HBM((R, COLS), jnp.float32),
            pltpu.HBM((1, ROWS, COLS), jnp.bfloat16),
        ],
        scratch_shapes=[
            pltpu.VMEM((count, R, WIDTH), jnp.float32),
            pltpu.VMEM((count, ROWS, WIDTH), jnp.bfloat16),
            pltpu.SemaphoreType.DMA((count,)),
            pltpu.SemaphoreType.DMA((count,)),
        ],
        input_output_aliases={count + 2 + i: i for i in range(len(so_far))},
        cost_estimate=pl.CostEstimate(flops=2 * count * ROWS * 6 * R * WIDTH, transcendentals=0,
                                      bytes_accessed=4 * count * (ROWS + R) * WIDTH),
        compiler_params=params(16),
        name="rewrite",
    )(*values, left, merged, *so_far)


def shift(value, axis, size, by):
    return lax.ppermute(value, axis, [(i, (i + by) % size) for i in range(size)])


def swap(value, axis, size):
    return lax.ppermute(value, axis, [(i, i ^ 1) for i in range(size)])


def ring4(value, axis, size, unit):
    across = shift(value, axis, size, 2 * unit)
    left = shift(value, axis, size, unit)
    right = shift(value, axis, size, size - unit)
    return (value + across) + (left + right)


def z_round(value, slot):
    pairs = []
    for z in range(NZ):
        for core in range(NC):
            by = Z_SHIFTS[core][slot]
            if by != 0:
                pairs.append((z * NC + core, (z + by) % NZ * NC + core))
    return lax.ppermute(value, ("z", "c"), pairs)


def exchange(value, axes):
    return lax.all_to_all(value, axes, 0, 0, tiled=True)


def x_ring(two, one, three):
    return shift(two, "x", NX, 2), shift(one, "x", NX, 1), shift(three, "x", NX, 3)


def on_device(grads, error, q_in):
    merged, term = merge(grads, error, q_in.T)
    own = term + swap(term, "c", NC)
    own = ring4(own, "y", NY, 1)
    own = ring4(own, "x", NX, 1)
    mine = [z_round(own, slot) for slot in range(SLOTS)]
    theirs = [swap(value, "c", NC) for value in mine]
    basis, p_half = orthonormal(own, mine, theirs)

    keep, send = right(p_half, merged, (2, 1, 3, 0))
    two, one, three, own = small(chip_sum_kernel, PARTS, NX, "chip_sum", keep, swap(send, "c", NC))
    [own] = small(x_sum_kernel, PARTS, 1, "x_sum", *x_ring(two, one, three), own)
    [mean] = small(mean_kernel, PARTS, 1, "mean", exchange(own, "z"))
    own = exchange(mean, "z")

    two, one, three = x_ring(own, own, own)
    left, p_basis = left_factor(basis)
    done = rewrite([(0, 0)], [own], left, merged, [])
    two, own, *done = lax.optimization_barrier((two, own, *done))
    far_two, far_own = swap(two, "c", NC), swap(own, "c", NC)
    done = rewrite([(2, 0)], [two], left, merged, done)
    three, one, *done = lax.optimization_barrier((three, one, *done))
    far_three, far_one = swap(three, "c", NC), swap(one, "c", NC)
    done = rewrite([(3, 0), (1, 0), (2, 1), (0, 1)], [three, one, far_two, far_own], left, merged, done)
    q_mean, new_error = rewrite([(3, 1), (1, 1)], [far_three, far_one], left, merged, done)
    return p_basis.T, q_mean.T, new_error


def solution(mesh):
    fine = Mesh(mesh.devices.reshape(NX, NZ, NC, NY), ("x", "z", "c", "y"))
    replicas = ("x", "z", "c")
    in_specs = (P(replicas, None, "y"), P(replicas, None, "y"), P("y", None))
    out_specs = (P(), P("y", None), P(replicas, None, "y"))
    return jax.shard_map(
        on_device, mesh=fine, in_specs=in_specs, out_specs=out_specs, check_vma=False
    )
```

```python
import jax
import jax.numpy as jnp
from jax import lax
from jax.experimental import pallas as pl
from jax.experimental.pallas import tpu as pltpu
from jax.sharding import Mesh, PartitionSpec as P

EPS = 1e-06
NX, NZ, NC, NY = 4, 8, 2, 4
ROWS, R, COLS = 256, 32, 7168
GROUP = R // NZ
BLOCK = COLS // NX
SLOTS = NZ // NC
WIDTH = BLOCK // NC
PARTS = (NZ, GROUP, WIDTH)
REPLICAS = NX * NZ * NC

VMEM = pl.BlockSpec(memory_space=pltpu.VMEM)
HBM = pl.BlockSpec(memory_space=pltpu.HBM)
CHUNK = 1024
CHUNKS = COLS // CHUNK
Z_SHIFTS = ((4, 3, 1, 0), (-3, 2, -2, -1))


def params(mib):
    return pltpu.CompilerParams(vmem_limit_bytes=mib * 1024 * 1024)


def merge_kernel(grads_ref, error_ref, q_ref, merged_ref, term_ref, g_buf, e_buf, q_buf, g_sem, e_sem, q_sem):
    def copies(i):
        columns = pl.ds(i * CHUNK, CHUNK)
        return (
            pltpu.make_async_copy(grads_ref.at[0, :, columns], g_buf.at[i], g_sem.at[i]),
            pltpu.make_async_copy(error_ref.at[0, :, columns], e_buf.at[i], e_sem.at[i]),
            pltpu.make_async_copy(q_ref.at[:, columns], q_buf.at[i], q_sem.at[i]),
        )

    for i in range(CHUNKS):
        for copy in copies(i):
            copy.start()
    total = jnp.zeros((R, ROWS), jnp.float32)
    for i in range(CHUNKS):
        for copy in copies(i):
            copy.wait()
        merged = (g_buf[i].astype(jnp.float32) + e_buf[i].astype(jnp.float32)).astype(jnp.bfloat16)
        merged_ref[:, i * CHUNK:(i + 1) * CHUNK] = merged
        total += lax.dot_general(q_buf[i].astype(jnp.bfloat16), merged, (((1,), (1,)), ((), ())),
                                 preferred_element_type=jnp.float32)
    term_ref[...] = total


def merge(grads, error, q_t):
    return pl.pallas_call(
        merge_kernel,
        in_specs=[HBM, HBM, HBM],
        out_specs=[VMEM, VMEM],
        out_shape=[
            pltpu.VMEM((ROWS, COLS), jnp.bfloat16),
            pltpu.VMEM((R, ROWS), jnp.float32),
        ],
        scratch_shapes=[
            pltpu.VMEM((CHUNKS, ROWS, CHUNK), jnp.bfloat16),
            pltpu.VMEM((CHUNKS, ROWS, CHUNK), jnp.bfloat16),
            pltpu.VMEM((CHUNKS, R, CHUNK), jnp.float32),
            pltpu.SemaphoreType.DMA((CHUNKS,)),
            pltpu.SemaphoreType.DMA((CHUNKS,)),
            pltpu.SemaphoreType.DMA((CHUNKS,)),
        ],
        compiler_params=params(24),
        name="merge",
    )(*(pltpu.with_memory_space_constraint(a, pltpu.HBM) for a in (grads, error, q_t)))


def tree(terms):
    while len(terms) > 1:
        terms = [a + b for a, b in zip(terms[::2], terms[1::2])]
    return terms[0]


def z_at(core, slot, sign):
    low, high = Z_SHIFTS[0][slot], Z_SHIFTS[1][slot]
    return (lax.axis_index("z") + jnp.where(core == 0, sign * low, sign * high) + NZ) % NZ


def orthonormal_kernel(own_ref, *refs):
    mine, theirs = refs[:SLOTS], refs[SLOTS:2 * SLOTS]
    basis_ref, half_ref, ring = refs[2 * SLOTS:]
    core = lax.axis_index("c")
    for group, owner in ((mine, core), (theirs, 1 - core)):
        for slot, ref in enumerate(group):
            ring[z_at(owner, slot, -1)] = ref[...]
    ring[lax.axis_index("z")] = own_ref[...]
    total = (ring[0] + ring[1]) + (ring[2] + ring[3])
    total = total + ((ring[4] + ring[5]) + (ring[6] + ring[7]))

    tiles = [total[8 * i:8 * i + 8] for i in range(R // 8)]
    left = list(tiles)
    basis = [jnp.zeros_like(tile) for tile in tiles]
    rows = lax.broadcasted_iota(jnp.int32, (8, 1), 0)
    for column in range(R):
        tile, row = divmod(column, 8)
        vector = left[tile][row:row + 1]
        if column > 0:
            built = (column - 1) // 8 + 1
            taken = None
            for part in basis[:built]:
                term = jnp.sum(part * vector, axis=1, keepdims=True) * part
                taken = term if taken is None else taken + term
            vector = vector - jnp.sum(taken, axis=0, keepdims=True)
        products = [jnp.sum(tiles[later] * vector, axis=1, keepdims=True) for later in range((column + 1) // 8, R // 8)]
        scale = lax.rsqrt(jnp.sum(vector * vector, axis=1, keepdims=True) + EPS)
        basis[tile] = jnp.where(rows == row, vector * scale, basis[tile])
        square = scale * scale
        for later, product in zip(range((column + 1) // 8, R // 8), products):
            left[later] = left[later] - (product * square) * vector
    result = jnp.concatenate(basis, axis=0)
    basis_ref[...] = result
    half_ref[...] = result.astype(jnp.bfloat16)


def small(kernel, out, count, name, *args, scratch=()):
    return pl.pallas_call(
        kernel,
        in_specs=[VMEM] * len(args),
        out_specs=[VMEM] * count,
        out_shape=[pltpu.VMEM(out, jnp.float32)] * count,
        scratch_shapes=list(scratch),
        compiler_params=params(16),
        name=name,
    )(*args)


def orthonormal(own, mine, theirs):
    return pl.pallas_call(
        orthonormal_kernel,
        in_specs=[VMEM] * (1 + 2 * SLOTS),
        out_specs=[VMEM, VMEM],
        out_shape=[
            pltpu.VMEM((R, ROWS), jnp.float32),
            pltpu.VMEM((R, ROWS), jnp.bfloat16),
        ],
        scratch_shapes=[pltpu.VMEM((NZ, R, ROWS), jnp.float32)],
        compiler_params=params(16),
        name="orthonormal",
    )(own, *mine, *theirs)


def right(p_half, merged, blocks_ahead):
    count = len(blocks_ahead)

    def kernel(half_ref, merged_ref, keep_ref, send_ref):
        first, x = lax.axis_index("c") == 0, lax.axis_index("x")
        for i, ahead in enumerate(blocks_ahead):
            columns = pl.ds(pl.multiple_of((x + ahead) % NX * BLOCK, 128), BLOCK)
            term = jnp.dot(half_ref[...], merged_ref[:, columns], preferred_element_type=jnp.float32)
            low, high = term[:, :WIDTH], term[:, WIDTH:]
            keep, send = jnp.where(first, low, high), jnp.where(first, high, low)
            for group in range(NZ):
                keep_ref[i, group] = keep[group * GROUP:(group + 1) * GROUP]
                send_ref[i, group] = send[group * GROUP:(group + 1) * GROUP]

    return small(kernel, (count,) + PARTS, 2, "right", p_half, merged)


def chip_sum_kernel(keep_ref, got_ref, *outs):
    for i, out in enumerate(outs):
        out[...] = keep_ref[i] + got_ref[i]


def x_sum_kernel(two_ref, one_ref, three_ref, own_ref, out_ref):
    out_ref[...] = (own_ref[...] + two_ref[...]) + (one_ref[...] + three_ref[...])


def mean_kernel(terms_ref, out_ref):
    total = tree([terms_ref[i] for i in range(NZ)]) * (1.0 / REPLICAS)
    for i in range(NZ):
        out_ref[i] = total


def split3(value):
    first = value.astype(jnp.bfloat16)
    rest = value - first.astype(jnp.float32)
    second = rest.astype(jnp.bfloat16)
    third = (rest - second.astype(jnp.float32)).astype(jnp.bfloat16)
    return first, second, third


def left_kernel(basis_ref, left_ref, out_ref, sem):
    copy = pltpu.make_async_copy(basis_ref, out_ref, sem)
    copy.start()
    p1, p2, p3 = split3(basis_ref[...])
    left_ref[...] = jnp.concatenate([p1, p1, p2, p2, p1, p3], axis=0).T
    copy.wait()


def left_factor(basis):
    return pl.pallas_call(
        left_kernel,
        in_specs=[VMEM],
        out_specs=[VMEM, HBM],
        out_shape=[pltpu.VMEM((ROWS, 6 * R), jnp.bfloat16), pltpu.HBM((R, ROWS), jnp.float32)],
        scratch_shapes=[pltpu.SemaphoreType.DMA],
        compiler_params=params(16),
        name="left_factor",
    )(basis)


def rewrite(places, values, left, merged, so_far):
    count = len(values)

    def kernel(*refs):
        held, (left_ref, merged_ref) = refs[:count], refs[count:count + 2]
        mean_ref, error_ref, mean_buf, error_buf, mean_sem, error_sem = refs[-6:]
        core, x = lax.axis_index("c"), lax.axis_index("x")
        copies = []
        for i, (behind, away) in enumerate(places):
            owner = 1 - core if away else core
            start = (x - behind + NX) % NX * BLOCK + owner * WIDTH
            columns = pl.ds(pl.multiple_of(start, 128), WIDTH)
            q_mean = jnp.concatenate([held[i][group] for group in range(NZ)], axis=0)
            mean_buf[i] = q_mean
            copies.append(pltpu.make_async_copy(mean_buf.at[i], mean_ref.at[:, columns], mean_sem.at[i]))
            copies[-1].start()
            q1, q2, q3 = split3(q_mean)
            q_all = jnp.concatenate([q1, q2, q1, q2, q3, q1], axis=0)
            for part in range(2):
                rows = slice(part * ROWS // 2, (part + 1) * ROWS // 2)
                approx = jnp.dot(left_ref[rows], q_all, preferred_element_type=jnp.float32)
                error_buf[i, rows] = (merged_ref[rows, columns].astype(jnp.float32) - approx).astype(jnp.bfloat16)
                copies.append(pltpu.make_async_copy(
                    error_buf.at[i, rows], error_ref.at[0, rows, columns], error_sem.at[2 * i + part]))
                copies[-1].start()
        for copy in copies:
            copy.wait()

    return pl.pallas_call(
        kernel,
        in_specs=[VMEM] * (count + 2) + [HBM] * len(so_far),
        out_specs=[HBM, HBM],
        out_shape=[
            pltpu.HBM((R, COLS), jnp.float32),
            pltpu.HBM((1, ROWS, COLS), jnp.bfloat16),
        ],
        scratch_shapes=[
            pltpu.VMEM((count, R, WIDTH), jnp.float32),
            pltpu.VMEM((count, ROWS, WIDTH), jnp.bfloat16),
            pltpu.SemaphoreType.DMA((count,)),
            pltpu.SemaphoreType.DMA((2 * count,)),
        ],
        input_output_aliases={count + 2 + i: i for i in range(len(so_far))},
        cost_estimate=pl.CostEstimate(flops=2 * count * ROWS * 6 * R * WIDTH, transcendentals=0,
                                      bytes_accessed=4 * count * (ROWS + R) * WIDTH),
        compiler_params=params(16),
        name="rewrite",
    )(*values, left, merged, *so_far)


def shift(value, axis, size, by):
    return lax.ppermute(value, axis, [(i, (i + by) % size) for i in range(size)])


def swap(value, axis, size):
    return lax.ppermute(value, axis, [(i, i ^ 1) for i in range(size)])


def ring4(value, axis, size, unit):
    across = shift(value, axis, size, 2 * unit)
    left = shift(value, axis, size, unit)
    right = shift(value, axis, size, size - unit)
    return (value + across) + (left + right)


def z_round(value, slot):
    pairs = []
    for z in range(NZ):
        for core in range(NC):
            by = Z_SHIFTS[core][slot]
            if by != 0:
                pairs.append((z * NC + core, (z + by) % NZ * NC + core))
    return lax.ppermute(value, ("z", "c"), pairs)


def exchange(value, axes):
    return lax.all_to_all(value, axes, 0, 0, tiled=True)


def x_ring(two, one, three):
    return shift(two, "x", NX, 2), shift(one, "x", NX, 1), shift(three, "x", NX, 3)


def on_device(grads, error, q_in):
    merged, term = merge(grads, error, q_in.T)
    own = term + swap(term, "c", NC)
    own = ring4(own, "y", NY, 1)
    own = ring4(own, "x", NX, 1)
    mine = [z_round(own, slot) for slot in range(SLOTS)]
    theirs = [swap(value, "c", NC) for value in mine]
    basis, p_half = orthonormal(own, mine, theirs)

    keep, send = right(p_half, merged, (2,))
    [two] = small(chip_sum_kernel, PARTS, 1, "chip_sum", keep, swap(send, "c", NC))
    two, p_half = lax.optimization_barrier((two, p_half))
    keep, send = right(p_half, merged, (1, 3, 0))
    one, three, own = small(chip_sum_kernel, PARTS, 3, "chip_sum", keep, swap(send, "c", NC))
    [own] = small(x_sum_kernel, PARTS, 1, "x_sum", *x_ring(two, one, three), own)
    [mean] = small(mean_kernel, PARTS, 1, "mean", exchange(own, "z"))
    own = exchange(mean, "z")

    two, one, three = x_ring(own, own, own)
    left, p_basis = left_factor(basis)
    done = rewrite([(0, 0)], [own], left, merged, [])
    two, own, *done = lax.optimization_barrier((two, own, *done))
    far_two, far_own = swap(two, "c", NC), swap(own, "c", NC)
    done = rewrite([(2, 0)], [two], left, merged, done)
    three, one, *done = lax.optimization_barrier((three, one, *done))
    far_three, far_one = swap(three, "c", NC), swap(one, "c", NC)
    done = rewrite([(3, 0), (1, 0), (2, 1), (0, 1)], [three, one, far_two, far_own], left, merged, done)
    q_mean, new_error = rewrite([(3, 1), (1, 1)], [far_three, far_one], left, merged, done)
    return p_basis.T, q_mean.T, new_error


def solution(mesh):
    fine = Mesh(mesh.devices.reshape(NX, NZ, NC, NY), ("x", "z", "c", "y"))
    replicas = ("x", "z", "c")
    in_specs = (P(replicas, None, "y"), P(replicas, None, "y"), P("y", None))
    out_specs = (P(), P("y", None), P(replicas, None, "y"))
    return jax.shard_map(
        on_device, mesh=fine, in_specs=in_specs, out_specs=out_specs, check_vma=False
    )
```
